32 devices in a mesh: box: 8 (over z, core), dir: 4 (over y, x).
Axes of the slice: x: 2, y: 2, z: 4, core: 2. Of those that a mesh axis runs over, the one named last changes fastest.
Arguments:
- fine_density: bfloat16 [1024, 1536], P(('box', 'dir')), may hold values from -6 to 6
- coarse_density: bfloat16 [512, 3072], P(('box', 'dir')), may hold values from -6 to 6
- fine_operators: bfloat16 [192, 3072], replicated, may hold values from -0.109375 to 0.109375
- coarse_operators: bfloat16 [192, 3072], replicated, may hold values from -0.109375 to 0.109375
- fine_balance: int32 [8], replicated, may hold values from 0 to 7, each once
- coarse_balance: int32 [16], replicated, may hold values from 0 to 15, each once
- fine_sources: int32 [8, 16384], P('dir', 'box'), may hold values from 0 to 1023, as said below
- fine_targets: int32 [8, 16384], P('dir', 'box'), may hold values from 0 to 1023, as said below
- fine_op_ids: int32 [8, 16384], P('dir', 'box'), may hold values from 0 to 15
- coarse_sources: int32 [16, 8192], P('dir', 'box'), may hold values from 0 to 511, as said below
- coarse_targets: int32 [16, 8192], P('dir', 'box'), may hold values from 0 to 511, as said below
- coarse_op_ids: int32 [16, 8192], P('dir', 'box'), may hold values from 0 to 15
Outputs:
- fine_local: bfloat16 [1024, 1536], P('box', 'dir')
- coarse_local: bfloat16 [512, 3072], P('box', 'dir')
The draws below stay inside these ranges and needn't reach their ends.
Inputs may be any that keep to these rules, and one draw needn't show every extreme that they name: `fine_targets`: pair column p belongs to the Morton range r = p // 2048; its target box lies in boxes r * 128 to (r + 1) * 128 - 1, and the first and last box of every range are named. `fine_sources`: the source of a pair of range r lies in boxes r * 128 - 32 to (r + 1) * 128 + 31, within the grid; in every range the sources at both ends of that span, as far as they lie in the grid, are named. `coarse_targets`: pair column p belongs to the Morton range r = p // 1024; its target box lies in boxes r * 64 to (r + 1) * 64 - 1, and the first and last box of every range are named. `coarse_sources`: the source of a pair of range r lies in boxes r * 64 - 32 to (r + 1) * 64 + 31, within the grid; in every range the sources at both ends of that span, as far as they lie in the grid, are named.
All inputs are finite; a program needn't handle non-finite values.
Results may differ from the reference program's by a relative error of at most 0.001.
Values may be sent and summed in bfloat16 or wider, within the bound.
A program may use at most 64 MiB of HBM per device.

```python
import jax
import jax.numpy as jnp
from jax import lax

C = 192
NOP = 16
PPB = 16
RIM = 32
BPB1 = 128
BPB2 = 64
NB1 = 1024
NB2 = 512
NW1 = 8
NW2 = 16
PAIRS1 = 16384
PAIRS2 = 8192


def target_draw(key, slots, pairs, per_range):
    column = jnp.arange(pairs, dtype=jnp.int32)
    lower = column // (PPB * per_range) * per_range
    within = column % (PPB * per_range)
    offsets = jax.random.randint(key, (slots, pairs), 0, per_range, dtype=jnp.int32)
    values = lower[None, :] + offsets
    values = jnp.where((within == 2)[None, :], (lower + per_range - 1)[None, :], values)
    values = jnp.where((within == 3)[None, :], lower[None, :], values)
    return values.astype(jnp.int32)


def source_draw(key, slots, pairs, per_range, total):
    column = jnp.arange(pairs, dtype=jnp.int32)
    lower = column // (PPB * per_range) * per_range
    within = column % (PPB * per_range)
    offsets = jax.random.randint(key, (slots, pairs), 0, per_range + 2 * RIM, dtype=jnp.int32)
    values = lower[None, :] - RIM + offsets
    values = jnp.where((within == 0)[None, :], (lower - RIM)[None, :], values)
    values = jnp.where((within == 1)[None, :], (lower + per_range + RIM - 1)[None, :], values)
    return jnp.clip(values, 0, total - 1).astype(jnp.int32)


def draw_fine_targets(key, part):
    return target_draw(jax.random.fold_in(key, 11), NW1, PAIRS1, BPB1)


def draw_fine_sources(key, part):
    return source_draw(jax.random.fold_in(key, 12), NW1, PAIRS1, BPB1, NB1)


def draw_coarse_targets(key, part):
    return target_draw(jax.random.fold_in(key, 13), NW2, PAIRS2, BPB2)


def draw_coarse_sources(key, part):
    return source_draw(jax.random.fold_in(key, 14), NW2, PAIRS2, BPB2, NB2)


def place_ends(drawn, stream_key, smallest, largest):
    extent = drawn.shape
    index_at = [jax.random.randint(jax.random.fold_in(stream_key, axis), (), 0, extent[axis]) for axis in range(len(extent))]
    drawn = drawn.at[tuple(index_at)].set(smallest)
    longest = extent.index(max(extent))
    index_at[longest] = (index_at[longest] + 1) % extent[longest]
    return drawn.at[tuple(index_at)].set(largest)


def level_of(stream_key, dims, shards, low, largest):
    def one(axis_at, parts):
        draws = jax.random.uniform(jax.random.fold_in(jax.random.fold_in(stream_key, 6), axis_at), (parts,), jnp.float32, low / len(shards), largest / len(shards))
        return jnp.repeat(jnp.exp(draws), dims[axis_at] // parts).reshape((-1,) + (1,) * (len(dims) - axis_at - 1))

    level = one(*shards[0])
    for cut in shards[1:]:
        level = level * one(*cut)
    return level


def noise(own_key, shape, deviation, bound, pieces=(), held_as=jnp.bfloat16):
    loudness = level_of(own_key, shape, pieces, -0.22, 0.18) if pieces else 1.0
    entries = jax.random.normal(own_key, shape, jnp.float32) * deviation * loudness
    return jnp.minimum(jnp.maximum(entries, -bound), bound).astype(held_as)


def setup_inputs(seed: int = 0) -> dict:
    key_of = jax.random.split(jax.random.key(seed), 13)
    return {
        "fine_density": noise(key_of[0], (NB1, NW1 * C), 1.0, 6.0, ((0, 32),)),
        "coarse_density": noise(key_of[1], (NB2, NW2 * C), 1.0, 6.0, ((0, 32),)),
        "fine_operators": noise(key_of[2], (C, NOP * C), (C * PPB) ** -0.5, 0.109375),
        "coarse_operators": noise(key_of[3], (C, NOP * C), (C * PPB) ** -0.5, 0.109375),
        "fine_balance": jax.random.permutation(key_of[4], NW1).astype(jnp.int32),
        "coarse_balance": jax.random.permutation(key_of[5], NW2).astype(jnp.int32),
        "fine_sources": draw_fine_sources(jax.random.fold_in(key_of[12], 71), 0),
        "fine_targets": draw_fine_targets(jax.random.fold_in(key_of[12], 71), 0),
        "fine_op_ids": place_ends(jax.random.randint(key_of[8], (NW1, PAIRS1), 0, NOP), jax.random.fold_in(key_of[8], 1), 0, NOP - 1).astype(jnp.int32),
        "coarse_sources": draw_coarse_sources(jax.random.fold_in(key_of[12], 71), 0),
        "coarse_targets": draw_coarse_targets(jax.random.fold_in(key_of[12], 71), 0),
        "coarse_op_ids": place_ends(jax.random.randint(key_of[11], (NW2, PAIRS2), 0, NOP), jax.random.fold_in(key_of[11], 1), 0, NOP - 1).astype(jnp.int32),
    }


def one_level(density, operators, balance, sources, targets, op_ids):
    channel = operators.shape[0]
    op_count = operators.shape[1] // channel
    box_count = density.shape[0]
    wedge_count = density.shape[1] // channel
    shaped = density.reshape(box_count, wedge_count, channel)
    sorted_slots = jnp.take(shaped, balance, axis=1)
    operators_wide = operators.astype(jnp.float32).reshape(channel, op_count, channel)

    def per_slot(packed):
        column, source_row, target_row, op_row = packed
        lookup = jnp.einsum("bc,cod->bod", column.astype(jnp.float32), operators_wide)
        picked = lookup.reshape(box_count * op_count, channel)[source_row * op_count + op_row]
        summed = jax.ops.segment_sum(picked, target_row, num_segments=box_count)
        return summed.astype(jnp.bfloat16)

    result = lax.map(per_slot, (jnp.transpose(sorted_slots, (1, 0, 2)), sources, targets, op_ids))
    return jnp.transpose(result, (1, 0, 2)).reshape(box_count, wedge_count * channel)


def reference(fine_density, coarse_density, fine_operators, coarse_operators, fine_balance, coarse_balance, fine_sources, fine_targets, fine_op_ids, coarse_sources, coarse_targets, coarse_op_ids):
    fine_local = one_level(fine_density, fine_operators, fine_balance, fine_sources, fine_targets, fine_op_ids)
    coarse_local = one_level(coarse_density, coarse_operators, coarse_balance, coarse_sources, coarse_targets, coarse_op_ids)
    return (fine_local, coarse_local)
```

```python
import functools

import jax
import jax.numpy as jnp
from jax import lax
from jax.experimental import pallas as pl
from jax.experimental.pallas import tpu as pltpu
from jax.sharding import PartitionSpec as P

RIM = 32
LANES = 128
BF16 = jnp.bfloat16
F32 = jnp.float32
MESH = pl.DeviceIdType.MESH


class Level:
    def __init__(self, density, operators, sources, nd):
        self.rows, width = density.shape
        self.channel = operators.shape[0]
        self.ops = operators.shape[1] // self.channel
        self.wedges = width // self.channel
        self.slots = self.wedges // nd
        self.targets = self.rows * nd
        self.halo = RIM // self.rows
        self.chunks = nd + 2 * self.halo
        self.span = self.targets + 2 * RIM
        self.pairs = sources.shape[1]
        self.full = self.span // LANES * LANES
        self.rest = self.span - self.full
        self.lo = 4 if self.rest else 2
        self.hi = self.ops // self.lo
        self.left = self.hi * self.targets
        self.right = self.lo * self.span
        self.depth = self.full + 2 * self.rest
        self.wide = -(-self.channel // LANES) * LANES


def one_hot(out, at, key, count):
    row = lax.broadcasted_iota(jnp.int32, (LANES, key.shape[1]), 0).astype(F32).astype(BF16)
    for base in range(0, count, LANES):
        near = (key - base).astype(F32).astype(BF16)
        hot = jnp.where(near == row, jnp.ones((), BF16), jnp.zeros((), BF16))
        out[base : base + LANES, :] = hot


def sort_slots(lv, nd, density, balance, split, send):
    for w in range(lv.wedges):
        split[w] = density[:, w * lv.channel : (w + 1) * lv.channel]
    for d in range(nd):
        parts = [split[balance[d * lv.slots + k]] for k in range(lv.slots)]
        send[d] = jnp.concatenate(parts, axis=1)


def copies(lv, nd, nb, b, d, send, ext, sems):
    send_sem, recv_sem = sems

    def copy(to_box, to_dir, chunk, sem):
        return pltpu.make_async_remote_copy(
            src_ref=send.at[to_dir],
            dst_ref=ext.at[chunk],
            send_sem=send_sem.at[sem],
            recv_sem=recv_sem.at[chunk],
            device_id=(to_box, to_dir),
            device_id_type=MESH,
        )

    sends, receives = [], []
    for step in range(nd):
        to = lax.rem(d + step, nd)
        up = jnp.logical_and(d >= nd - lv.halo, b < nb - 1)
        down = jnp.logical_and(d < lv.halo, b > 0)
        if step:
            sends.append((None, functools.partial(copy, b, to, lv.halo + d, step)))
        sends.append((up, functools.partial(copy, b + 1, to, d - (nd - lv.halo), nd + step)))
        sends.append((down, functools.partial(copy, b - 1, to, lv.halo + nd + d, 2 * nd + step)))
    for step in range(1, nd):
        chunk = lv.halo + lax.rem(d + step, nd)
        receives.append((None, functools.partial(copy, b, d, chunk, 0)))
    for i in range(lv.halo):
        receives.append((b > 0, functools.partial(copy, b, d, i, 0)))
        receives.append((b < nb - 1, functools.partial(copy, b, d, lv.halo + nd + i, 0)))
    return sends, receives


def under(condition, act):
    if condition is None:
        act()
    else:
        pl.when(condition)(act)


def histogram(lv, b, sources, targets, op_ids, left, right, counts):
    def body(j, _):
        at = pl.ds(j, 1)
        op = op_ids[at, :]
        high, low = op // lv.lo, op % lv.lo
        source = sources[at, :] - (b * lv.targets - RIM)
        target = targets[at, :] - b * lv.targets
        key = low * lv.full + source
        if lv.rest:
            tail = lv.lo * lv.full + low * lv.rest + (source - lv.full)
            key = jnp.where(source < lv.full, key, tail)
        one_hot(left, None, high * lv.targets + target, lv.left)
        one_hot(right, None, key, lv.right)
        found = lax.dot_general(
            left[...], right[...], (((1,), (1,)), ((), ())), preferred_element_type=F32
        )
        main = found.astype(BF16)
        counts[j, 0] = main
        counts[j, 1] = (found - main.astype(F32)).astype(BF16)
        return 0

    lax.fori_loop(0, lv.slots, body, 0)


def gather_rows(lv, ext, flat, weights):
    for q in range(lv.chunks):
        flat[q * lv.rows : (q + 1) * lv.rows, :] = ext[q].astype(flat.dtype)
    for j in range(lv.slots):
        mine = flat[:, j * lv.channel : (j + 1) * lv.channel].astype(BF16)
        pad = jnp.zeros((lv.span, lv.wide - lv.channel), BF16)
        mine = jnp.concatenate([mine, pad], axis=1)
        if lv.rest:
            none = jnp.zeros((lv.rest, lv.wide), BF16)
            weights[j, 0] = jnp.concatenate([mine, none], axis=0)
            weights[j, 1] = jnp.concatenate([mine[: lv.full], none, mine[lv.full :]], axis=0)
        else:
            weights[j, 0] = mine


def expand(lv, counts, weights, grown):
    def body(j, _):
        for low in range(lv.lo):
            picked = []
            for term in range(2):
                for k in range(lv.full // LANES):
                    first = low * lv.full + k * LANES
                    picked.append(counts[j, term, :, first : first + LANES])
                if lv.rest:
                    first = lv.lo * lv.full + (low // 2) * LANES
                    picked.append(counts[j, term, :, first : first + LANES])
            weight = weights[j, low % 2 if lv.rest else 0]
            total = jnp.dot(
                jnp.concatenate(picked, axis=1),
                jnp.concatenate([weight, weight], axis=0),
                preferred_element_type=F32,
            )
            main = total.astype(BF16)
            rest = (total - main.astype(F32)).astype(BF16)
            for high in range(lv.hi):
                op = high * lv.lo + low
                column = op // 2 * lv.wide
                rows = slice(high * lv.targets, (high + 1) * lv.targets)
                grown[op % 2, j, : lv.targets, column : column + lv.wide] = main[rows]
                grown[op % 2, j, lv.targets :, column : column + lv.wide] = rest[rows]
        return 0

    lax.fori_loop(0, lv.slots, body, 0)


def apply_operators(lv, grown, table, out):
    height = lv.slots * 2 * lv.targets
    total = []
    for parity in range(2):
        total.append(
            jnp.dot(
                grown[parity].reshape(height, grown.shape[-1]),
                table[parity],
                preferred_element_type=F32,
            )
        )
    shift = lv.wide - lv.channel
    both = total[0][:, : lv.channel] + total[1][:, shift:]
    parts = []
    for j in range(lv.slots):
        first = j * 2 * lv.targets
        part = both[first : first + lv.targets] + both[first + lv.targets : first + 2 * lv.targets]
        parts.append(part.astype(BF16))
    out[...] = jnp.concatenate(parts, axis=1)


def operator_copies(lv, operators, table, sem):
    shift = lv.wide - lv.channel
    result = []
    for op in range(lv.ops):
        first = op * lv.channel - (op % 2) * shift
        result.append(
            pltpu.make_async_copy(
                operators.at[:, pl.ds(first, lv.wide)],
                table.at[op % 2, pl.ds(op // 2 * lv.wide, lv.channel), :],
                sem.at[op],
            )
        )
    return result


def kernel(levels, nd, nb, *refs):
    (dens1, dens2, oper1, oper2, bal1, bal2, src1, tgt1, ids1, src2, tgt2, ids2, out1, out2) = refs[:14]
    scratch = refs[14:]
    per = len(scratch) // 2
    sets = (scratch[:per], scratch[per:])
    data = (
        (dens1, oper1, bal1, src1, tgt1, ids1, out1),
        (dens2, oper2, bal2, src2, tgt2, ids2, out2),
    )
    b, d = lax.axis_index("box"), lax.axis_index("dir")

    barrier = pltpu.get_barrier_semaphore()
    for step in range(1, nd):
        pl.semaphore_signal(barrier, inc=1, device_id=(b, lax.rem(d + step, nd)), device_id_type=MESH)

    @pl.when(b > 0)
    def _():
        for to in range(nd):
            pl.semaphore_signal(barrier, inc=1, device_id=(b - 1, to), device_id_type=MESH)

    @pl.when(b < nb - 1)
    def _():
        for to in range(nd):
            pl.semaphore_signal(barrier, inc=1, device_id=(b + 1, to), device_id_type=MESH)

    loads = []
    for lv, (_, oper, *_), s in zip(levels, data, sets):
        loads += operator_copies(lv, oper, s[8], s[11])
    for load in loads:
        load.start()

    for lv, (dens, _, bal, *_), s in zip(levels, data, sets):
        sort_slots(lv, nd, dens, bal, s[0], s[1])

    sides = 1 + (b > 0).astype(jnp.int32) + (b < nb - 1).astype(jnp.int32)
    pl.semaphore_wait(barrier, sides * nd - 1)

    plans = []
    for lv, s in zip(levels, sets):
        send, ext = s[1], s[2]
        sends, receives = copies(lv, nd, nb, b, d, send, ext, (s[9], s[10]))
        plans.append((sends, receives))
        for condition, make in sends:
            under(condition, lambda make=make: make().start())

    for lv, (_, _, _, src, tgt, ids, _), s in zip(levels, data, sets):
        send, ext, left, right, counts = s[1], s[2], s[4], s[5], s[6]
        ext[lv.halo + d] = send[d]
        blank = jnp.zeros(ext.shape[1:], BF16)

        @pl.when(b == 0)
        def _():
            for i in range(lv.halo):
                ext[i] = blank

        @pl.when(b == nb - 1)
        def _():
            for i in range(lv.halo):
                ext[lv.halo + nd + i] = blank

        table = s[8]
        hole = jnp.zeros((lv.wide - lv.channel, lv.wide), BF16)
        for parity in range(2):
            for k in range(lv.ops // 2):
                table[parity, k * lv.wide + lv.channel : (k + 1) * lv.wide, :] = hole
        histogram(lv, b, src, tgt, ids, left, right, counts)

    for sends, receives in plans:
        for condition, make in receives:
            under(condition, lambda make=make: make().wait_recv())
    for load in loads:
        load.wait()

    for lv, (*_, out), s in zip(levels, data, sets):
        gather_rows(lv, s[2], s[3], s[7])
        expand(lv, s[6], s[7], s[12])
        apply_operators(lv, s[12], s[8], out)

    for sends, receives in plans:
        for condition, make in sends:
            under(condition, lambda make=make: make().wait_send())


def scratch_of(lv, nd):
    flat = BF16 if lv.rows % 16 == 0 else F32
    width = lv.slots * lv.channel
    return [
        pltpu.VMEM((lv.wedges, lv.rows, lv.channel), BF16),
        pltpu.VMEM((nd, lv.rows, width), BF16),
        pltpu.VMEM((lv.chunks, lv.rows, width), BF16),
        pltpu.VMEM((lv.span, width), flat),
        pltpu.VMEM((lv.left, lv.pairs), BF16),
        pltpu.VMEM((lv.right, lv.pairs), BF16),
        pltpu.VMEM((lv.slots, 2, lv.left, lv.right), BF16),
        pltpu.VMEM((lv.slots, 2 if lv.rest else 1, lv.depth, lv.wide), BF16),
        pltpu.VMEM((2, lv.ops // 2 * lv.wide, lv.wide), BF16),
        pltpu.SemaphoreType.DMA((3 * nd,)),
        pltpu.SemaphoreType.DMA((lv.chunks,)),
        pltpu.SemaphoreType.DMA((lv.ops,)),
        pltpu.VMEM((2, lv.slots, 2 * lv.targets, lv.ops // 2 * lv.wide), BF16),
    ]


def per_device(nd, nb, *args):
    fine = Level(args[0], args[2], args[6], nd)
    coarse = Level(args[1], args[3], args[9], nd)
    levels = (fine, coarse)
    vmem = pl.BlockSpec(memory_space=pltpu.VMEM)
    smem = pl.BlockSpec(memory_space=pltpu.SMEM)
    away = pl.BlockSpec(memory_space=pl.ANY)
    return pl.pallas_call(
        functools.partial(kernel, levels, nd, nb),
        out_shape=tuple(
            jax.ShapeDtypeStruct((lv.targets, lv.slots * lv.channel), BF16) for lv in levels
        ),
        in_specs=[vmem, vmem, away, away, smem, smem] + [vmem] * 6,
        out_specs=(vmem, vmem),
        scratch_shapes=scratch_of(fine, nd) + scratch_of(coarse, nd),
        compiler_params=pltpu.CompilerParams(
            collective_id=0, has_side_effects=True, vmem_limit_bytes=56 * 1024 * 1024
        ),
        name="translate",
    )(*args)


def solution(mesh):
    boxes, dirs = P(("box", "dir"), None), P("dir", "box")
    return jax.shard_map(
        functools.partial(per_device, mesh.shape["dir"], mesh.shape["box"]),
        mesh=mesh,
        in_specs=(boxes, boxes, P(), P(), P(), P()) + (dirs,) * 6,
        out_specs=(P("box", "dir"), P("box", "dir")),
        check_vma=False,
    )
```

```python
import functools

import jax
import jax.numpy as jnp
from jax import lax
from jax.experimental import pallas as pl
from jax.experimental.pallas import tpu as pltpu
from jax.sharding import PartitionSpec as P

RIM = 32
LANES = 128
BF16 = jnp.bfloat16
F32 = jnp.float32
MESH = pl.DeviceIdType.MESH


class Level:
    def __init__(self, density, operators, sources, nd):
        self.rows, width = density.shape
        self.channel = operators.shape[0]
        self.ops = operators.shape[1] // self.channel
        self.wedges = width // self.channel
        self.slots = self.wedges // nd
        self.targets = self.rows * nd
        self.halo = RIM // self.rows
        self.chunks = nd + 2 * self.halo
        self.span = self.targets + 2 * RIM
        self.pairs = sources.shape[1]
        self.full = self.span // LANES * LANES
        self.rest = self.span - self.full
        self.lo = 4 if self.rest else 2
        self.hi = self.ops // self.lo
        self.left = self.hi * self.targets
        self.right = self.lo * self.span
        self.depth = self.full + 2 * self.rest
        self.wide = -(-self.channel // LANES) * LANES


def one_hot(out, key, count):
    row = lax.broadcasted_iota(jnp.int32, (LANES, key.shape[1]), 0).astype(F32).astype(BF16)
    block = (key // LANES).astype(F32).astype(BF16)
    within = (key % LANES).astype(F32).astype(BF16)
    for base in range(0, count, LANES):
        near = jnp.where(block == jnp.asarray(base // LANES, BF16), within, -jnp.ones((), BF16))
        hot = jnp.where(near == row, jnp.ones((), BF16), jnp.zeros((), BF16))
        out[base : base + LANES, :] = hot


def sort_slots(lv, nd, density, balance, split, send):
    for w in range(lv.wedges):
        split[w] = density[:, w * lv.channel : (w + 1) * lv.channel]
    for d in range(nd):
        parts = [split[balance[d * lv.slots + k]] for k in range(lv.slots)]
        send[d] = jnp.concatenate(parts, axis=1)


def copies(lv, nd, nb, b, d, send, ext, sems):
    send_sem, recv_sem = sems

    def copy(to_box, to_dir, chunk, sem):
        return pltpu.make_async_remote_copy(
            src_ref=send.at[to_dir],
            dst_ref=ext.at[chunk],
            send_sem=send_sem.at[sem],
            recv_sem=recv_sem.at[chunk],
            device_id=(to_box, to_dir),
            device_id_type=MESH,
        )

    sends, receives = [], []
    for step in range(nd):
        to = lax.rem(d + step, nd)
        up = jnp.logical_and(d >= nd - lv.halo, b < nb - 1)
        down = jnp.logical_and(d < lv.halo, b > 0)
        if step:
            sends.append((None, functools.partial(copy, b, to, lv.halo + d, step)))
        sends.append((up, functools.partial(copy, b + 1, to, d - (nd - lv.halo), nd + step)))
        sends.append((down, functools.partial(copy, b - 1, to, lv.halo + nd + d, 2 * nd + step)))
    for step in range(1, nd):
        chunk = lv.halo + lax.rem(d + step, nd)
        receives.append((None, functools.partial(copy, b, d, chunk, 0)))
    for i in range(lv.halo):
        receives.append((b > 0, functools.partial(copy, b, d, i, 0)))
        receives.append((b < nb - 1, functools.partial(copy, b, d, lv.halo + nd + i, 0)))
    return sends, receives


def under(condition, act):
    if condition is None:
        act()
    else:
        pl.when(condition)(act)


def histogram(lv, b, sources, targets, op_ids, left, right, counts):
    def body(j, _):
        at = pl.ds(j, 1)
        op = op_ids[at, :]
        high, low = op // lv.lo, op % lv.lo
        source = sources[at, :] - (b * lv.targets - RIM)
        target = targets[at, :] - b * lv.targets
        key = low * lv.full + source
        if lv.rest:
            tail = lv.lo * lv.full + low * lv.rest + (source - lv.full)
            key = jnp.where(source < lv.full, key, tail)
        one_hot(left, high * lv.targets + target, lv.left)
        one_hot(right, key, lv.right)
        found = lax.dot_general(
            left[...], right[...], (((1,), (1,)), ((), ())), preferred_element_type=F32
        )
        main = found.astype(BF16)
        counts[j, 0] = main
        counts[j, 1] = (found - main.astype(F32)).astype(BF16)
        return 0

    lax.fori_loop(0, lv.slots, body, 0)


def gather_rows(lv, ext, flat, weights):
    for q in range(lv.chunks):
        flat[q * lv.rows : (q + 1) * lv.rows, :] = ext[q].astype(flat.dtype)
    for j in range(lv.slots):
        mine = flat[:, j * lv.channel : (j + 1) * lv.channel].astype(BF16)
        pad = jnp.zeros((lv.span, lv.wide - lv.channel), BF16)
        mine = jnp.concatenate([mine, pad], axis=1)
        if lv.rest:
            none = jnp.zeros((lv.rest, lv.wide), BF16)
            weights[j, 0] = jnp.concatenate([mine, none], axis=0)
            weights[j, 1] = jnp.concatenate([mine[: lv.full], none, mine[lv.full :]], axis=0)
        else:
            weights[j, 0] = mine


def expand(lv, counts, weights, grown):
    def body(j, _):
        for low in range(lv.lo):
            picked = []
            for term in range(2):
                for k in range(lv.full // LANES):
                    first = low * lv.full + k * LANES
                    picked.append(counts[j, term, :, first : first + LANES])
                if lv.rest:
                    first = lv.lo * lv.full + (low // 2) * LANES
                    picked.append(counts[j, term, :, first : first + LANES])
            weight = weights[j, low % 2 if lv.rest else 0]
            total = jnp.dot(
                jnp.concatenate(picked, axis=1),
                jnp.concatenate([weight, weight], axis=0),
                preferred_element_type=F32,
            )
            main = total.astype(BF16)
            rest = (total - main.astype(F32)).astype(BF16)
            for high in range(lv.hi):
                op = high * lv.lo + low
                column = op // 2 * lv.wide
                rows = slice(high * lv.targets, (high + 1) * lv.targets)
                grown[op % 2, j, : lv.targets, column : column + lv.wide] = main[rows]
                grown[op % 2, j, lv.targets :, column : column + lv.wide] = rest[rows]
        return 0

    lax.fori_loop(0, lv.slots, body, 0)


def apply_operators(lv, grown, table, out):
    height = lv.slots * 2 * lv.targets
    total = []
    for parity in range(2):
        total.append(
            jnp.dot(
                grown[parity].reshape(height, grown.shape[-1]),
                table[parity],
                preferred_element_type=F32,
            )
        )
    shift = lv.wide - lv.channel
    both = total[0][:, : lv.channel] + total[1][:, shift:]
    parts = []
    for j in range(lv.slots):
        first = j * 2 * lv.targets
        part = both[first : first + lv.targets] + both[first + lv.targets : first + 2 * lv.targets]
        parts.append(part.astype(BF16))
    out[...] = jnp.concatenate(parts, axis=1)


def operator_copies(lv, operators, table, sem):
    shift = lv.wide - lv.channel
    result = []
    for op in range(lv.ops):
        first = op * lv.channel - (op % 2) * shift
        result.append(
            pltpu.make_async_copy(
                operators.at[:, pl.ds(first, lv.wide)],
                table.at[op % 2, pl.ds(op // 2 * lv.wide, lv.channel), :],
                sem.at[op],
            )
        )
    return result


def kernel(levels, nd, nb, *refs):
    (dens1, dens2, oper1, oper2, bal1, bal2, src1, tgt1, ids1, src2, tgt2, ids2, out1, out2) = refs[:14]
    scratch = refs[14:]
    per = len(scratch) // 2
    sets = (scratch[:per], scratch[per:])
    data = (
        (dens1, oper1, bal1, src1, tgt1, ids1, out1),
        (dens2, oper2, bal2, src2, tgt2, ids2, out2),
    )
    b, d = lax.axis_index("box"), lax.axis_index("dir")

    firsts = []
    for (dens, _, _, src, tgt, ids, _), s in zip(data, sets):
        moves = zip((dens, src, tgt, ids), s[14:18])
        firsts.append([pltpu.make_async_copy(a, v, s[13].at[i]) for i, (a, v) in enumerate(moves)])
    for i in range(4):
        for first in firsts:
            first[i].start()

    barrier = pltpu.get_barrier_semaphore()
    for step in range(1, nd):
        pl.semaphore_signal(barrier, inc=1, device_id=(b, lax.rem(d + step, nd)), device_id_type=MESH)

    @pl.when(b > 0)
    def _():
        for to in range(nd):
            pl.semaphore_signal(barrier, inc=1, device_id=(b - 1, to), device_id_type=MESH)

    @pl.when(b < nb - 1)
    def _():
        for to in range(nd):
            pl.semaphore_signal(barrier, inc=1, device_id=(b + 1, to), device_id_type=MESH)

    loads = []
    for lv, (_, oper, *_), s in zip(levels, data, sets):
        loads += operator_copies(lv, oper, s[8], s[11])
    for load in loads:
        load.start()

    for lv, (_, _, bal, *_), s, first in zip(levels, data, sets, firsts):
        first[0].wait()
        sort_slots(lv, nd, s[14], bal, s[0], s[1])

    sides = 1 + (b > 0).astype(jnp.int32) + (b < nb - 1).astype(jnp.int32)
    pl.semaphore_wait(barrier, sides * nd - 1)

    plans = []
    for lv, s in zip(levels, sets):
        send, ext = s[1], s[2]
        sends, receives = copies(lv, nd, nb, b, d, send, ext, (s[9], s[10]))
        plans.append((sends, receives))
        for condition, make in sends:
            under(condition, lambda make=make: make().start())

    for lv, s, waits in zip(levels, sets, firsts):
        src, tgt, ids = s[15:18]
        send, ext, left, right, counts = s[1], s[2], s[4], s[5], s[6]
        for wait in waits[1:]:
            wait.wait()
        ext[lv.halo + d] = send[d]
        blank = jnp.zeros(ext.shape[1:], BF16)

        @pl.when(b == 0)
        def _():
            for i in range(lv.halo):
                ext[i] = blank

        @pl.when(b == nb - 1)
        def _():
            for i in range(lv.halo):
                ext[lv.halo + nd + i] = blank

        table = s[8]
        hole = jnp.zeros((lv.wide - lv.channel, lv.wide), BF16)
        for parity in range(2):
            for k in range(lv.ops // 2):
                table[parity, k * lv.wide + lv.channel : (k + 1) * lv.wide, :] = hole
        histogram(lv, b, src, tgt, ids, left, right, counts)

    for sends, receives in plans:
        for condition, make in receives:
            under(condition, lambda make=make: make().wait_recv())
    for load in loads:
        load.wait()

    results = []
    for lv, (*_, out), s in zip(levels, data, sets):
        gather_rows(lv, s[2], s[3], s[7])
        expand(lv, s[6], s[7], s[12])
        apply_operators(lv, s[12], s[8], s[18])
        results.append(pltpu.make_async_copy(s[18], out, s[13].at[4]))
        results[-1].start()

    for sends, receives in plans:
        for condition, make in sends:
            under(condition, lambda make=make: make().wait_send())
    for result in results:
        result.wait()


def hand_on(one, two, out1, out2, sem):
    moves = [
        pltpu.make_async_copy(one, out1, sem.at[0]),
        pltpu.make_async_copy(two, out2, sem.at[1]),
    ]
    for move in moves:
        move.start()
    for move in moves:
        move.wait()


def scratch_of(lv, nd):
    flat = BF16 if lv.rows % 16 == 0 else F32
    width = lv.slots * lv.channel
    return [
        pltpu.VMEM((lv.wedges, lv.rows, lv.channel), BF16),
        pltpu.VMEM((nd, lv.rows, width), BF16),
        pltpu.VMEM((lv.chunks, lv.rows, width), BF16),
        pltpu.VMEM((lv.span, width), flat),
        pltpu.VMEM((lv.left, lv.pairs), BF16),
        pltpu.VMEM((lv.right, lv.pairs), BF16),
        pltpu.VMEM((lv.slots, 2, lv.left, lv.right), BF16),
        pltpu.VMEM((lv.slots, 2 if lv.rest else 1, lv.depth, lv.wide), BF16),
        pltpu.VMEM((2, lv.ops // 2 * lv.wide, lv.wide), BF16),
        pltpu.SemaphoreType.DMA((3 * nd,)),
        pltpu.SemaphoreType.DMA((lv.chunks,)),
        pltpu.SemaphoreType.DMA((lv.ops,)),
        pltpu.VMEM((2, lv.slots, 2 * lv.targets, lv.ops // 2 * lv.wide), BF16),
        pltpu.SemaphoreType.DMA((5,)),
        pltpu.VMEM((lv.rows, lv.wedges * lv.channel), BF16),
        pltpu.VMEM((lv.slots, lv.pairs), jnp.int32),
        pltpu.VMEM((lv.slots, lv.pairs), jnp.int32),
        pltpu.VMEM((lv.slots, lv.pairs), jnp.int32),
        pltpu.VMEM((lv.targets, width), BF16),
    ]


def per_device(nd, nb, *args):
    fine = Level(args[0], args[2], args[6], nd)
    coarse = Level(args[1], args[3], args[9], nd)
    levels = (fine, coarse)
    smem = pl.BlockSpec(memory_space=pltpu.SMEM)
    away = pl.BlockSpec(memory_space=pl.ANY)
    shapes = tuple(
        jax.ShapeDtypeStruct((lv.targets, lv.slots * lv.channel), BF16) for lv in levels
    )
    found = pl.pallas_call(
        functools.partial(kernel, levels, nd, nb),
        out_shape=shapes,
        in_specs=[away] * 4 + [smem] * 2 + [away] * 6,
        out_specs=(away, away),
        scratch_shapes=scratch_of(fine, nd) + scratch_of(coarse, nd),
        compiler_params=pltpu.CompilerParams(
            collective_id=0, has_side_effects=True, vmem_limit_bytes=56 * 1024 * 1024
        ),
        name="translate",
    )(*args)
    return pl.pallas_call(
        hand_on,
        out_shape=shapes,
        in_specs=[away] * 2,
        out_specs=(away, away),
        scratch_shapes=[pltpu.SemaphoreType.DMA((2,))],
        compiler_params=pltpu.CompilerParams(vmem_limit_bytes=60 * 1024 * 1024),
        name="hand_on",
    )(*found)


def solution(mesh):
    boxes, dirs = P(("box", "dir"), None), P("dir", "box")
    return jax.shard_map(
        functools.partial(per_device, mesh.shape["dir"], mesh.shape["box"]),
        mesh=mesh,
        in_specs=(boxes, boxes, P(), P(), P(), P()) + (dirs,) * 6,
        out_specs=(P("box", "dir"), P("box", "dir")),
        check_vma=False,
    )
```

```python
import functools

import jax
import jax.numpy as jnp
from jax import lax
from jax.experimental import pallas as pl
from jax.experimental.pallas import tpu as pltpu
from jax.sharding import PartitionSpec as P

RIM = 32
LANES = 128
BF16 = jnp.bfloat16
F32 = jnp.float32
HOT = jnp.float8_e4m3fn
MESH = pl.DeviceIdType.MESH


class Level:
    def __init__(self, density, operators, sources, nd):
        self.rows, width = density.shape
        self.channel = operators.shape[0]
        self.ops = operators.shape[1] // self.channel
        self.wedges = width // self.channel
        self.slots = self.wedges // nd
        self.targets = self.rows * nd
        self.halo = RIM // self.rows
        self.chunks = nd + 2 * self.halo
        self.span = self.targets + 2 * RIM
        self.pairs = sources.shape[1]
        self.full = self.span // LANES * LANES
        self.rest = self.span - self.full
        self.lo = 4 if self.rest else 2
        self.hi = self.ops // self.lo
        self.left = self.hi * self.targets
        self.right = self.lo * self.span
        self.depth = self.full + 2 * self.rest
        self.wide = -(-self.channel // LANES) * LANES


def one_hot(out, key, count):
    row = lax.broadcasted_iota(jnp.int32, (LANES, key.shape[1]), 0).astype(F32).astype(BF16)
    block = (key // LANES).astype(F32).astype(BF16)
    within = (key % LANES).astype(F32).astype(BF16)
    for base in range(0, count, LANES):
        near = jnp.where(block == jnp.asarray(base // LANES, BF16), within, -jnp.ones((), BF16))
        hot = jnp.where(near == row, jnp.ones((), BF16), jnp.zeros((), BF16))
        out[base : base + LANES, :] = hot.astype(out.dtype)


def sort_slots(lv, nd, density, balance, split, send):
    for w in range(lv.wedges):
        split[w] = density[:, w * lv.channel : (w + 1) * lv.channel]
    for d in range(nd):
        parts = [split[balance[d * lv.slots + k]] for k in range(lv.slots)]
        send[d] = jnp.concatenate(parts, axis=1)


def copies(lv, nd, nb, b, d, send, ext, sems):
    send_sem, recv_sem = sems

    def copy(to_box, to_dir, chunk, sem):
        return pltpu.make_async_remote_copy(
            src_ref=send.at[to_dir],
            dst_ref=ext.at[chunk],
            send_sem=send_sem.at[sem],
            recv_sem=recv_sem.at[chunk],
            device_id=(to_box, to_dir),
            device_id_type=MESH,
        )

    sends, receives = [], []
    for step in range(nd):
        to = lax.rem(d + step, nd)
        up = jnp.logical_and(d >= nd - lv.halo, b < nb - 1)
        down = jnp.logical_and(d < lv.halo, b > 0)
        if step:
            sends.append((None, functools.partial(copy, b, to, lv.halo + d, step)))
        sends.append((up, functools.partial(copy, b + 1, to, d - (nd - lv.halo), nd + step)))
        sends.append((down, functools.partial(copy, b - 1, to, lv.halo + nd + d, 2 * nd + step)))
    for step in range(1, nd):
        chunk = lv.halo + lax.rem(d + step, nd)
        receives.append((None, functools.partial(copy, b, d, chunk, 0)))
    for i in range(lv.halo):
        receives.append((b > 0, functools.partial(copy, b, d, i, 0)))
        receives.append((b < nb - 1, functools.partial(copy, b, d, lv.halo + nd + i, 0)))
    return sends, receives


def under(condition, act):
    if condition is None:
        act()
    else:
        pl.when(condition)(act)


def histogram(lv, b, sources, targets, op_ids, left, right, counts):
    def body(j, _):
        at = pl.ds(j, 1)
        op = op_ids[at, :]
        high, low = op // lv.lo, op % lv.lo
        source = sources[at, :] - (b * lv.targets - RIM)
        target = targets[at, :] - b * lv.targets
        key = low * lv.full + source
        if lv.rest:
            tail = lv.lo * lv.full + low * lv.rest + (source - lv.full)
            key = jnp.where(source < lv.full, key, tail)
        one_hot(left, high * lv.targets + target, lv.left)
        one_hot(right, key, lv.right)
        found = lax.dot_general(
            left[...], right[...], (((1,), (1,)), ((), ())), preferred_element_type=F32
        )
        main = found.astype(BF16)
        counts[j, 0] = main
        counts[j, 1] = (found - main.astype(F32)).astype(BF16)
        return 0

    lax.fori_loop(0, lv.slots, body, 0)


def gather_rows(lv, ext, flat, weights):
    for q in range(lv.chunks):
        flat[q * lv.rows : (q + 1) * lv.rows, :] = ext[q].astype(flat.dtype)
    for j in range(lv.slots):
        mine = flat[:, j * lv.channel : (j + 1) * lv.channel].astype(BF16)
        pad = jnp.zeros((lv.span, lv.wide - lv.channel), BF16)
        mine = jnp.concatenate([mine, pad], axis=1)
        if lv.rest:
            none = jnp.zeros((lv.rest, lv.wide), BF16)
            weights[j, 0] = jnp.concatenate([mine, none], axis=0)
            weights[j, 1] = jnp.concatenate([mine[: lv.full], none, mine[lv.full :]], axis=0)
        else:
            weights[j, 0] = mine


def expand(lv, counts, weights, grown):
    def body(j, _):
        for low in range(lv.lo):
            picked = []
            for term in range(2):
                for k in range(lv.full // LANES):
                    first = low * lv.full + k * LANES
                    picked.append(counts[j, term, :, first : first + LANES])
                if lv.rest:
                    first = lv.lo * lv.full + (low // 2) * LANES
                    picked.append(counts[j, term, :, first : first + LANES])
            weight = weights[j, low % 2 if lv.rest else 0]
            total = jnp.dot(
                jnp.concatenate(picked, axis=1),
                jnp.concatenate([weight, weight], axis=0),
                preferred_element_type=F32,
            )
            main = total.astype(BF16)
            rest = (total - main.astype(F32)).astype(BF16)
            for high in range(lv.hi):
                op = high * lv.lo + low
                column = op // 2 * lv.wide
                rows = slice(high * lv.targets, (high + 1) * lv.targets)
                grown[op % 2, j, : lv.targets, column : column + lv.wide] = main[rows]
                grown[op % 2, j, lv.targets :, column : column + lv.wide] = rest[rows]
        return 0

    lax.fori_loop(0, lv.slots, body, 0)


def apply_operators(lv, grown, table, out):
    height = lv.slots * 2 * lv.targets
    total = []
    for parity in range(2):
        total.append(
            jnp.dot(
                grown[parity].reshape(height, grown.shape[-1]),
                table[parity],
                preferred_element_type=F32,
            )
        )
    shift = lv.wide - lv.channel
    both = total[0][:, : lv.channel] + total[1][:, shift:]
    parts = []
    for j in range(lv.slots):
        first = j * 2 * lv.targets
        part = both[first : first + lv.targets] + both[first + lv.targets : first + 2 * lv.targets]
        parts.append(part.astype(BF16))
    out[...] = jnp.concatenate(parts, axis=1)


def operator_copies(lv, operators, table, sem):
    shift = lv.wide - lv.channel
    result = []
    for op in range(lv.ops):
        first = op * lv.channel - (op % 2) * shift
        result.append(
            pltpu.make_async_copy(
                operators.at[:, pl.ds(first, lv.wide)],
                table.at[op % 2, pl.ds(op // 2 * lv.wide, lv.channel), :],
                sem.at[op],
            )
        )
    return result


def kernel(levels, nd, nb, *refs):
    (dens1, dens2, oper1, oper2, bal1, bal2, src1, tgt1, ids1, src2, tgt2, ids2, out1, out2) = refs[:14]
    scratch = refs[14:]
    per = len(scratch) // 2
    sets = (scratch[:per], scratch[per:])
    data = (
        (dens1, oper1, bal1, src1, tgt1, ids1, out1),
        (dens2, oper2, bal2, src2, tgt2, ids2, out2),
    )
    b, d = lax.axis_index("box"), lax.axis_index("dir")

    firsts = []
    for (dens, _, _, src, tgt, ids, _), s in zip(data, sets):
        moves = zip((dens, src, tgt, ids), s[14:18])
        firsts.append([pltpu.make_async_copy(a, v, s[13].at[i]) for i, (a, v) in enumerate(moves)])
    for i in range(4):
        for first in firsts:
            first[i].start()

    barrier = pltpu.get_barrier_semaphore()
    for step in range(1, nd):
        pl.semaphore_signal(barrier, inc=1, device_id=(b, lax.rem(d + step, nd)), device_id_type=MESH)

    @pl.when(b > 0)
    def _():
        for to in range(nd):
            pl.semaphore_signal(barrier, inc=1, device_id=(b - 1, to), device_id_type=MESH)

    @pl.when(b < nb - 1)
    def _():
        for to in range(nd):
            pl.semaphore_signal(barrier, inc=1, device_id=(b + 1, to), device_id_type=MESH)

    loads = []
    for lv, (_, oper, *_), s in zip(levels, data, sets):
        loads += operator_copies(lv, oper, s[8], s[11])
    for load in loads:
        load.start()

    for lv, (_, _, bal, *_), s, first in zip(levels, data, sets, firsts):
        first[0].wait()
        sort_slots(lv, nd, s[14], bal, s[0], s[1])

    sides = 1 + (b > 0).astype(jnp.int32) + (b < nb - 1).astype(jnp.int32)
    pl.semaphore_wait(barrier, sides * nd - 1)

    plans = []
    for lv, s in zip(levels, sets):
        send, ext = s[1], s[2]
        sends, receives = copies(lv, nd, nb, b, d, send, ext, (s[9], s[10]))
        plans.append((sends, receives))
        for condition, make in sends:
            under(condition, lambda make=make: make().start())

    for lv, s, waits in zip(levels, sets, firsts):
        src, tgt, ids = s[15:18]
        send, ext, left, right, counts = s[1], s[2], s[4], s[5], s[6]
        for wait in waits[1:]:
            wait.wait()
        ext[lv.halo + d] = send[d]
        blank = jnp.zeros(ext.shape[1:], BF16)

        @pl.when(b == 0)
        def _():
            for i in range(lv.halo):
                ext[i] = blank

        @pl.when(b == nb - 1)
        def _():
            for i in range(lv.halo):
                ext[lv.halo + nd + i] = blank

        table = s[8]
        hole = jnp.zeros((lv.wide - lv.channel, lv.wide), BF16)
        for parity in range(2):
            for k in range(lv.ops // 2):
                table[parity, k * lv.wide + lv.channel : (k + 1) * lv.wide, :] = hole
        histogram(lv, b, src, tgt, ids, left, right, counts)

    for sends, receives in plans:
        for condition, make in receives:
            under(condition, lambda make=make: make().wait_recv())
    for load in loads:
        load.wait()

    results = []
    for lv, (*_, out), s in zip(levels, data, sets):
        gather_rows(lv, s[2], s[3], s[7])
        expand(lv, s[6], s[7], s[12])
        apply_operators(lv, s[12], s[8], s[18])
        results.append(pltpu.make_async_copy(s[18], out, s[13].at[4]))
        results[-1].start()

    for sends, receives in plans:
        for condition, make in sends:
            under(condition, lambda make=make: make().wait_send())
    for result in results:
        result.wait()


def hand_on(one, two, out1, out2):
    out1[...] = one[...]
    out2[...] = two[...]


def scratch_of(lv, nd):
    flat = BF16 if lv.rows % 16 == 0 else F32
    width = lv.slots * lv.channel
    return [
        pltpu.VMEM((lv.wedges, lv.rows, lv.channel), BF16),
        pltpu.VMEM((nd, lv.rows, width), BF16),
        pltpu.VMEM((lv.chunks, lv.rows, width), BF16),
        pltpu.VMEM((lv.span, width), flat),
        pltpu.VMEM((lv.left, lv.pairs), HOT),
        pltpu.VMEM((lv.right, lv.pairs), HOT),
        pltpu.VMEM((lv.slots, 2, lv.left, lv.right), BF16),
        pltpu.VMEM((lv.slots, 2 if lv.rest else 1, lv.depth, lv.wide), BF16),
        pltpu.VMEM((2, lv.ops // 2 * lv.wide, lv.wide), BF16),
        pltpu.SemaphoreType.DMA((3 * nd,)),
        pltpu.SemaphoreType.DMA((lv.chunks,)),
        pltpu.SemaphoreType.DMA((lv.ops,)),
        pltpu.VMEM((2, lv.slots, 2 * lv.targets, lv.ops // 2 * lv.wide), BF16),
        pltpu.SemaphoreType.DMA((5,)),
        pltpu.VMEM((lv.rows, lv.wedges * lv.channel), BF16),
        pltpu.VMEM((lv.slots, lv.pairs), jnp.int32),
        pltpu.VMEM((lv.slots, lv.pairs), jnp.int32),
        pltpu.VMEM((lv.slots, lv.pairs), jnp.int32),
        pltpu.VMEM((lv.targets, width), BF16),
    ]


def per_device(nd, nb, *args):
    fine = Level(args[0], args[2], args[6], nd)
    coarse = Level(args[1], args[3], args[9], nd)
    levels = (fine, coarse)
    smem = pl.BlockSpec(memory_space=pltpu.SMEM)
    away = pl.BlockSpec(memory_space=pl.ANY)
    shapes = tuple(
        jax.ShapeDtypeStruct((lv.targets, lv.slots * lv.channel), BF16) for lv in levels
    )
    found = pl.pallas_call(
        functools.partial(kernel, levels, nd, nb),
        out_shape=shapes,
        in_specs=[away] * 4 + [smem] * 2 + [away] * 6,
        out_specs=(away, away),
        scratch_shapes=scratch_of(fine, nd) + scratch_of(coarse, nd),
        compiler_params=pltpu.CompilerParams(
            collective_id=0, has_side_effects=True, vmem_limit_bytes=56 * 1024 * 1024
        ),
        name="translate",
    )(*args)
    return pl.pallas_call(
        hand_on,
        out_shape=shapes,
        compiler_params=pltpu.CompilerParams(vmem_limit_bytes=60 * 1024 * 1024),
        name="hand_on",
    )(*found)


def solution(mesh):
    boxes, dirs = P(("box", "dir"), None), P("dir", "box")
    return jax.shard_map(
        functools.partial(per_device, mesh.shape["dir"], mesh.shape["box"]),
        mesh=mesh,
        in_specs=(boxes, boxes, P(), P(), P(), P()) + (dirs,) * 6,
        out_specs=(P("box", "dir"), P("box", "dir")),
        check_vma=False,
    )
```

```python
import functools

import jax
import jax.numpy as jnp
from jax import lax
from jax.experimental import pallas as pl
from jax.experimental.pallas import tpu as pltpu
from jax.sharding import PartitionSpec as P

RIM = 32
LANES = 128
BF16 = jnp.bfloat16
F32 = jnp.float32
HOT = jnp.float8_e4m3fn
MESH = pl.DeviceIdType.MESH


class Level:
    def __init__(self, density, operators, sources, nd):
        self.rows, width = density.shape
        self.channel = operators.shape[0]
        self.ops = operators.shape[1] // self.channel
        self.wedges = width // self.channel
        self.slots = self.wedges // nd
        self.targets = self.rows * nd
        self.halo = RIM // self.rows
        self.chunks = nd + 2 * self.halo
        self.span = self.targets + 2 * RIM
        self.pairs = sources.shape[1]
        self.full = self.span // LANES * LANES
        self.rest = self.span - self.full
        self.lo = 4 if self.rest else 2
        self.hi = self.ops // self.lo
        self.left = self.hi * self.targets
        self.right = self.lo * self.span
        self.depth = self.full + 2 * self.rest
        self.wide = -(-self.channel // LANES) * LANES


def one_hot_pieces(out, key, count):
    row = lax.broadcasted_iota(jnp.int32, (LANES, LANES), 0).astype(F32).astype(BF16)
    row = jnp.concatenate([row] * (key.shape[1] // LANES), axis=1)
    block = lax.shift_right_logical(key, LANES.bit_length() - 1).astype(F32).astype(BF16)
    within = jnp.bitwise_and(key, LANES - 1).astype(F32).astype(BF16)

    def piece(k):
        near = jnp.where(block == jnp.asarray(k, BF16), within, -jnp.ones((), BF16))
        hot = jnp.where(near == row, jnp.ones((), BF16), jnp.zeros((), BF16))
        out[k * LANES : (k + 1) * LANES, :] = hot.astype(out.dtype)

    return [functools.partial(piece, k) for k in range(count // LANES)]


def sort_slots(lv, nd, density, balance, split, send):
    for w in range(lv.wedges):
        split[w] = density[:, w * lv.channel : (w + 1) * lv.channel]
    for d in range(nd):
        parts = [split[balance[d * lv.slots + k]] for k in range(lv.slots)]
        send[d] = jnp.concatenate(parts, axis=1)


def copies(lv, nd, nb, b, d, send, ext, sems):
    send_sem, recv_sem = sems

    def copy(to_box, to_dir, chunk, sem):
        return pltpu.make_async_remote_copy(
            src_ref=send.at[to_dir],
            dst_ref=ext.at[chunk],
            send_sem=send_sem.at[sem],
            recv_sem=recv_sem.at[chunk],
            device_id=(to_box, to_dir),
            device_id_type=MESH,
        )

    sends, receives = [], []
    for step in range(nd):
        to = lax.rem(d + step, nd)
        up = jnp.logical_and(d >= nd - lv.halo, b < nb - 1)
        down = jnp.logical_and(d < lv.halo, b > 0)
        if step:
            sends.append((None, functools.partial(copy, b, to, lv.halo + d, step)))
        sends.append((up, functools.partial(copy, b + 1, to, d - (nd - lv.halo), nd + step)))
        sends.append((down, functools.partial(copy, b - 1, to, lv.halo + nd + d, 2 * nd + step)))
    for step in range(1, nd):
        chunk = lv.halo + lax.rem(d + step, nd)
        receives.append((None, functools.partial(copy, b, d, chunk, 0)))
    for i in range(lv.halo):
        receives.append((b > 0, functools.partial(copy, b, d, i, 0)))
        receives.append((b < nb - 1, functools.partial(copy, b, d, lv.halo + nd + i, 0)))
    return sends, receives


def under(condition, act):
    if condition is None:
        act()
    else:
        pl.when(condition)(act)


def hot_pieces(lv, b, j, sources, targets, op_ids, left, right):
    at = slice(j, j + 1)
    op = op_ids[at, :]
    high = lax.shift_right_logical(op, lv.lo.bit_length() - 1)
    low = jnp.bitwise_and(op, lv.lo - 1)
    source = sources[at, :] - (b * lv.targets - RIM)
    target = targets[at, :] - b * lv.targets
    key = low * lv.full + source
    if lv.rest:
        tail = lv.lo * lv.full + low * lv.rest + (source - lv.full)
        key = jnp.where(source < lv.full, key, tail)
    return one_hot_pieces(left, high * lv.targets + target, lv.left) + one_hot_pieces(
        right, key, lv.right
    )


def count_pieces(lv, j, left, right, counts):
    def piece(columns):
        found = lax.dot_general(
            left[...], right[columns, :], (((1,), (1,)), ((), ())), preferred_element_type=F32
        )
        main = found.astype(BF16)
        counts[j, 0, :, columns] = main
        counts[j, 1, :, columns] = (found - main.astype(F32)).astype(BF16)

    step = 2 * LANES
    return [functools.partial(piece, slice(c, c + step)) for c in range(0, lv.right, step)]


def interleave(first, second):
    done = 0
    for i, act in enumerate(second):
        until = (i + 1) * len(first) // len(second)
        for other in first[done:until]:
            other()
        done = until
        act()
    for other in first[done:]:
        other()


def gather_rows(lv, ext, flat, weights):
    for q in range(lv.chunks):
        flat[q * lv.rows : (q + 1) * lv.rows, :] = ext[q].astype(flat.dtype)
    for j in range(lv.slots):
        mine = flat[:, j * lv.channel : (j + 1) * lv.channel].astype(BF16)
        pad = jnp.zeros((lv.span, lv.wide - lv.channel), BF16)
        mine = jnp.concatenate([mine, pad], axis=1)
        if lv.rest:
            none = jnp.zeros((lv.rest, lv.wide), BF16)
            weights[j, 0] = jnp.concatenate([mine, none], axis=0)
            weights[j, 1] = jnp.concatenate([mine[: lv.full], none, mine[lv.full :]], axis=0)
        else:
            weights[j, 0] = mine


def expand(lv, counts, weights, grown):
    def body(j):
        for low in range(lv.lo):
            picked = []
            for term in range(2):
                for k in range(lv.full // LANES):
                    first = low * lv.full + k * LANES
                    picked.append(counts[j, term, :, first : first + LANES])
                if lv.rest:
                    first = lv.lo * lv.full + (low // 2) * LANES
                    picked.append(counts[j, term, :, first : first + LANES])
            weight = weights[j, low % 2 if lv.rest else 0]
            total = jnp.dot(
                jnp.concatenate(picked, axis=1),
                jnp.concatenate([weight, weight], axis=0),
                preferred_element_type=F32,
            )
            main = total.astype(BF16)
            rest = (total - main.astype(F32)).astype(BF16)
            for high in range(lv.hi):
                op = high * lv.lo + low
                column = op // 2 * lv.wide
                rows = slice(high * lv.targets, (high + 1) * lv.targets)
                grown[op % 2, j, : lv.targets, column : column + lv.wide] = main[rows]
                grown[op % 2, j, lv.targets :, column : column + lv.wide] = rest[rows]

    for j in range(lv.slots):
        body(j)


def apply_operators(lv, grown, table, out):
    height = lv.slots * 2 * lv.targets
    total = []
    for parity in range(2):
        total.append(
            jnp.dot(
                grown[parity].reshape(height, grown.shape[-1]),
                table[parity],
                preferred_element_type=F32,
            )
        )
    shift = lv.wide - lv.channel
    both = total[0][:, : lv.channel] + total[1][:, shift:]
    parts = []
    for j in range(lv.slots):
        first = j * 2 * lv.targets
        part = both[first : first + lv.targets] + both[first + lv.targets : first + 2 * lv.targets]
        parts.append(part.astype(BF16))
    out[...] = jnp.concatenate(parts, axis=1)


def operator_copies(lv, operators, table, sem):
    shift = lv.wide - lv.channel
    result = []
    for op in range(lv.ops):
        first = op * lv.channel - (op % 2) * shift
        result.append(
            pltpu.make_async_copy(
                operators.at[:, pl.ds(first, lv.wide)],
                table.at[op % 2, pl.ds(op // 2 * lv.wide, lv.channel), :],
                sem.at[op],
            )
        )
    return result


def kernel(levels, nd, nb, *refs):
    (dens1, dens2, oper1, oper2, bal1, bal2, src1, tgt1, ids1, src2, tgt2, ids2, out1, out2) = refs[:14]
    scratch = refs[14:]
    per = len(scratch) // 2
    sets = (scratch[:per], scratch[per:])
    data = (
        (dens1, oper1, bal1, src1, tgt1, ids1, out1),
        (dens2, oper2, bal2, src2, tgt2, ids2, out2),
    )
    b, d = lax.axis_index("box"), lax.axis_index("dir")

    firsts = []
    for (dens, _, _, src, tgt, ids, _), s in zip(data, sets):
        moves = zip((dens, src, tgt, ids), s[14:18])
        firsts.append([pltpu.make_async_copy(a, v, s[13].at[i]) for i, (a, v) in enumerate(moves)])
    for i in range(4):
        for first in firsts:
            first[i].start()

    barrier = pltpu.get_barrier_semaphore()
    for step in range(1, nd):
        pl.semaphore_signal(barrier, inc=1, device_id=(b, lax.rem(d + step, nd)), device_id_type=MESH)

    @pl.when(b > 0)
    def _():
        for to in range(nd):
            pl.semaphore_signal(barrier, inc=1, device_id=(b - 1, to), device_id_type=MESH)

    @pl.when(b < nb - 1)
    def _():
        for to in range(nd):
            pl.semaphore_signal(barrier, inc=1, device_id=(b + 1, to), device_id_type=MESH)

    tables = []
    for lv, (_, oper, *_), s in zip(levels, data, sets):
        tables.append(operator_copies(lv, oper, s[8], s[11]))
        for load in tables[-1]:
            load.start()

    for lv, (_, _, bal, *_), s, first in zip(levels, data, sets, firsts):
        first[0].wait()
        sort_slots(lv, nd, s[14], bal, s[0], s[1])

    sides = 1 + (b > 0).astype(jnp.int32) + (b < nb - 1).astype(jnp.int32)
    pl.semaphore_wait(barrier, sides * nd - 1)

    plans = []
    for lv, s in zip(levels, sets):
        send, ext = s[1], s[2]
        sends, receives = copies(lv, nd, nb, b, d, send, ext, (s[9], s[10]))
        plans.append((sends, receives))
        for condition, make in sends:
            under(condition, lambda make=make: make().start())

    jobs = []
    for lv, s, waits in zip(levels, sets, firsts):
        src, tgt, ids = s[15:18]
        send, ext, lefts, rights, counts = s[1], s[2], s[4], s[5], s[6]
        for wait in waits[1:]:
            wait.wait()
        ext[lv.halo + d] = send[d]
        blank = jnp.zeros(ext.shape[1:], BF16)

        @pl.when(b == 0)
        def _():
            for i in range(lv.halo):
                ext[i] = blank

        @pl.when(b == nb - 1)
        def _():
            for i in range(lv.halo):
                ext[lv.halo + nd + i] = blank

        table = s[8]
        hole = jnp.zeros((lv.wide - lv.channel, lv.wide), BF16)
        for parity in range(2):
            for k in range(lv.ops // 2):
                table[parity, k * lv.wide + lv.channel : (k + 1) * lv.wide, :] = hole
        for j in range(lv.slots):
            left, right = lefts.at[j % 2], rights.at[j % 2]
            jobs.append(
                (
                    functools.partial(hot_pieces, lv, b, j, src, tgt, ids, left, right),
                    functools.partial(count_pieces, lv, j, left, right, counts),
                )
            )

    for act in jobs[0][0]():
        act()
    for i, (_, count) in enumerate(jobs):
        interleave(jobs[i + 1][0]() if i + 1 < len(jobs) else [], count())

    results = []
    for lv, (*_, out), s, (_, receives), loads in zip(levels, data, sets, plans, tables):
        for condition, make in receives:
            under(condition, lambda make=make: make().wait_recv())
        for load in loads:
            load.wait()
        gather_rows(lv, s[2], s[3], s[7])
        expand(lv, s[6], s[7], s[12])
        apply_operators(lv, s[12], s[8], s[18])
        results.append(pltpu.make_async_copy(s[18], out, s[13].at[4]))
        results[-1].start()

    for sends, receives in plans:
        for condition, make in sends:
            under(condition, lambda make=make: make().wait_send())
    for result in results:
        result.wait()


def hand_on(one, two, out1, out2):
    out1[...] = one[...]
    out2[...] = two[...]


def scratch_of(lv, nd):
    flat = BF16 if lv.rows % 16 == 0 else F32
    width = lv.slots * lv.channel
    return [
        pltpu.VMEM((lv.wedges, lv.rows, lv.channel), BF16),
        pltpu.VMEM((nd, lv.rows, width), BF16),
        pltpu.VMEM((lv.chunks, lv.rows, width), BF16),
        pltpu.VMEM((lv.span, width), flat),
        pltpu.VMEM((2, lv.left, lv.pairs), HOT),
        pltpu.VMEM((2, lv.right, lv.pairs), HOT),
        pltpu.VMEM((lv.slots, 2, lv.left, lv.right), BF16),
        pltpu.VMEM((lv.slots, 2 if lv.rest else 1, lv.depth, lv.wide), BF16),
        pltpu.VMEM((2, lv.ops // 2 * lv.wide, lv.wide), BF16),
        pltpu.SemaphoreType.DMA((3 * nd,)),
        pltpu.SemaphoreType.DMA((lv.chunks,)),
        pltpu.SemaphoreType.DMA((lv.ops,)),
        pltpu.VMEM((2, lv.slots, 2 * lv.targets, lv.ops // 2 * lv.wide), BF16),
        pltpu.SemaphoreType.DMA((5,)),
        pltpu.VMEM((lv.rows, lv.wedges * lv.channel), BF16),
        pltpu.VMEM((lv.slots, lv.pairs), jnp.int32),
        pltpu.VMEM((lv.slots, lv.pairs), jnp.int32),
        pltpu.VMEM((lv.slots, lv.pairs), jnp.int32),
        pltpu.VMEM((lv.targets, width), BF16),
    ]


def per_device(nd, nb, *args):
    fine = Level(args[0], args[2], args[6], nd)
    coarse = Level(args[1], args[3], args[9], nd)
    levels = (fine, coarse)
    smem = pl.BlockSpec(memory_space=pltpu.SMEM)
    away = pl.BlockSpec(memory_space=pl.ANY)
    shapes = tuple(
        jax.ShapeDtypeStruct((lv.targets, lv.slots * lv.channel), BF16) for lv in levels
    )
    found = pl.pallas_call(
        functools.partial(kernel, levels, nd, nb),
        out_shape=shapes,
        in_specs=[away] * 4 + [smem] * 2 + [away] * 6,
        out_specs=(away, away),
        scratch_shapes=scratch_of(fine, nd) + scratch_of(coarse, nd),
        compiler_params=pltpu.CompilerParams(
            collective_id=0, has_side_effects=True, vmem_limit_bytes=56 * 1024 * 1024
        ),
        name="translate",
    )(*args)
    return pl.pallas_call(
        hand_on,
        out_shape=shapes,
        compiler_params=pltpu.CompilerParams(vmem_limit_bytes=60 * 1024 * 1024),
        name="hand_on",
    )(*found)


def solution(mesh):
    boxes, dirs = P(("box", "dir"), None), P("dir", "box")
    return jax.shard_map(
        functools.partial(per_device, mesh.shape["dir"], mesh.shape["box"]),
        mesh=mesh,
        in_specs=(boxes, boxes, P(), P(), P(), P()) + (dirs,) * 6,
        out_specs=(P("box", "dir"), P("box", "dir")),
        check_vma=False,
    )
```

```python
import functools

import jax
import jax.numpy as jnp
from jax import lax
from jax.experimental import pallas as pl
from jax.experimental.pallas import tpu as pltpu
from jax.sharding import PartitionSpec as P

RIM = 32
LANES = 128
BF16 = jnp.bfloat16
F32 = jnp.float32
HOT = jnp.float8_e4m3fn
MESH = pl.DeviceIdType.MESH


class Level:
    def __init__(self, density, operators, sources, nd):
        self.rows, width = density.shape
        self.channel = operators.shape[0]
        self.ops = operators.shape[1] // self.channel
        self.wedges = width // self.channel
        self.slots = self.wedges // nd
        self.targets = self.rows * nd
        self.halo = RIM // self.rows
        self.chunks = nd + 2 * self.halo
        self.span = self.targets + 2 * RIM
        self.pairs = sources.shape[1]
        self.full = self.span // LANES * LANES
        self.rest = self.span - self.full
        self.lo = 4 if self.rest else 2
        self.hi = self.ops // self.lo
        self.left = self.hi * self.targets
        self.right = self.lo * self.span
        self.depth = self.full + 2 * self.rest
        self.wide = -(-self.channel // LANES) * LANES


def one_hot_pieces(out, key, count):
    row = lax.broadcasted_iota(jnp.int32, (LANES, LANES), 0).astype(F32).astype(BF16)
    row = jnp.concatenate([row] * (key.shape[1] // LANES), axis=1)
    block = lax.shift_right_logical(key, LANES.bit_length() - 1).astype(F32).astype(BF16)
    within = jnp.bitwise_and(key, LANES - 1).astype(F32).astype(BF16)

    def piece(k):
        near = jnp.where(block == jnp.asarray(k, BF16), within, -jnp.ones((), BF16))
        hot = jnp.where(near == row, jnp.ones((), BF16), jnp.zeros((), BF16))
        out[k * LANES : (k + 1) * LANES, :] = hot.astype(out.dtype)

    return [functools.partial(piece, k) for k in range(count // LANES)]


def sort_slots(lv, nd, density, balance, split, send):
    for w in range(lv.wedges):
        split[w] = density[:, w * lv.channel : (w + 1) * lv.channel]
    for d in range(nd):
        parts = [split[balance[d * lv.slots + k]] for k in range(lv.slots)]
        send[d] = jnp.concatenate(parts, axis=1)


def exchange(lv, nd, b, d, send, ext, send_sem, recv_sem):
    result = []
    for step in range(1, nd):
        to = lax.rem(d + step, nd)
        result.append(
            pltpu.make_async_remote_copy(
                src_ref=send.at[to],
                dst_ref=ext.at[lv.halo + d],
                send_sem=send_sem.at[step],
                recv_sem=recv_sem.at[nd - step],
                device_id=(b, to),
                device_id_type=MESH,
            )
        )
    return result


def halo_copies(lv, nd, nb, b, d, ext, sem):
    up = pltpu.make_async_remote_copy(
        src_ref=ext.at[pl.ds(nd, lv.halo)],
        dst_ref=ext.at[pl.ds(0, lv.halo)],
        send_sem=sem.at[0],
        recv_sem=sem.at[1],
        device_id=(b + 1, d),
        device_id_type=MESH,
    )
    down = pltpu.make_async_remote_copy(
        src_ref=ext.at[pl.ds(lv.halo, lv.halo)],
        dst_ref=ext.at[pl.ds(lv.halo + nd, lv.halo)],
        send_sem=sem.at[2],
        recv_sem=sem.at[3],
        device_id=(b - 1, d),
        device_id_type=MESH,
    )
    return [(b < nb - 1, b > 0, up), (b > 0, b < nb - 1, down)]


def hot_pieces(lv, b, j, sources, targets, op_ids, left, right):
    at = slice(j, j + 1)
    op = op_ids[at, :]
    high = lax.shift_right_logical(op, lv.lo.bit_length() - 1)
    low = jnp.bitwise_and(op, lv.lo - 1)
    source = sources[at, :] - (b * lv.targets - RIM)
    target = targets[at, :] - b * lv.targets
    key = low * lv.full + source
    if lv.rest:
        tail = lv.lo * lv.full + low * lv.rest + (source - lv.full)
        key = jnp.where(source < lv.full, key, tail)
    return one_hot_pieces(left, high * lv.targets + target, lv.left) + one_hot_pieces(
        right, key, lv.right
    )


def count_pieces(lv, j, left, right, counts):
    def piece(columns):
        found = lax.dot_general(
            left[...], right[columns, :], (((1,), (1,)), ((), ())), preferred_element_type=F32
        )
        main = found.astype(BF16)
        counts[j, 0, :, columns] = main
        counts[j, 1, :, columns] = (found - main.astype(F32)).astype(BF16)

    step = 2 * LANES
    return [functools.partial(piece, slice(c, c + step)) for c in range(0, lv.right, step)]


def interleave(first, second):
    done = 0
    for i, act in enumerate(second):
        until = (i + 1) * len(first) // len(second)
        for other in first[done:until]:
            other()
        done = until
        act()
    for other in first[done:]:
        other()


def gather_rows(lv, ext, flat, weights):
    for q in range(lv.chunks):
        flat[q * lv.rows : (q + 1) * lv.rows, :] = ext[q].astype(flat.dtype)
    for j in range(lv.slots):
        mine = flat[:, j * lv.channel : (j + 1) * lv.channel].astype(BF16)
        pad = jnp.zeros((lv.span, lv.wide - lv.channel), BF16)
        mine = jnp.concatenate([mine, pad], axis=1)
        if lv.rest:
            none = jnp.zeros((lv.rest, lv.wide), BF16)
            weights[j, 0] = jnp.concatenate([mine, none], axis=0)
            weights[j, 1] = jnp.concatenate([mine[: lv.full], none, mine[lv.full :]], axis=0)
        else:
            weights[j, 0] = mine


def expand(lv, counts, weights, grown):
    def body(j):
        for low in range(lv.lo):
            picked = []
            for term in range(2):
                for k in range(lv.full // LANES):
                    first = low * lv.full + k * LANES
                    picked.append(counts[j, term, :, first : first + LANES])
                if lv.rest:
                    first = lv.lo * lv.full + (low // 2) * LANES
                    picked.append(counts[j, term, :, first : first + LANES])
            weight = weights[j, low % 2 if lv.rest else 0]
            total = jnp.dot(
                jnp.concatenate(picked, axis=1),
                jnp.concatenate([weight, weight], axis=0),
                preferred_element_type=F32,
            )
            main = total.astype(BF16)
            rest = (total - main.astype(F32)).astype(BF16)
            for high in range(lv.hi):
                op = high * lv.lo + low
                column = op // 2 * lv.wide
                rows = slice(high * lv.targets, (high + 1) * lv.targets)
                grown[op % 2, j, : lv.targets, column : column + lv.wide] = main[rows]
                grown[op % 2, j, lv.targets :, column : column + lv.wide] = rest[rows]

    for j in range(lv.slots):
        body(j)


def apply_operators(lv, grown, table, out):
    height = lv.slots * 2 * lv.targets
    total = []
    for parity in range(2):
        total.append(
            jnp.dot(
                grown[parity].reshape(height, grown.shape[-1]),
                table[parity],
                preferred_element_type=F32,
            )
        )
    shift = lv.wide - lv.channel
    both = total[0][:, : lv.channel] + total[1][:, shift:]
    parts = []
    for j in range(lv.slots):
        first = j * 2 * lv.targets
        part = both[first : first + lv.targets] + both[first + lv.targets : first + 2 * lv.targets]
        parts.append(part.astype(BF16))
    out[...] = jnp.concatenate(parts, axis=1)


def operator_copies(lv, operators, table, sem):
    shift = lv.wide - lv.channel
    result = []
    for op in range(lv.ops):
        first = op * lv.channel - (op % 2) * shift
        result.append(
            pltpu.make_async_copy(
                operators.at[:, pl.ds(first, lv.wide)],
                table.at[op % 2, pl.ds(op // 2 * lv.wide, lv.channel), :],
                sem.at[op],
            )
        )
    return result


def kernel(levels, nd, nb, *refs):
    (dens1, dens2, oper1, oper2, bal1, bal2, src1, tgt1, ids1, src2, tgt2, ids2, out1, out2) = refs[:14]
    scratch = refs[14:]
    per = len(scratch) // 2
    sets = (scratch[:per], scratch[per:])
    data = (
        (dens1, oper1, bal1, src1, tgt1, ids1, out1),
        (dens2, oper2, bal2, src2, tgt2, ids2, out2),
    )
    fine_slots, coarse_slots = (lv.slots for lv in levels)
    b, d = lax.axis_index("box"), lax.axis_index("dir")

    firsts = []
    for (dens, _, _, src, tgt, ids, _), s in zip(data, sets):
        moves = zip((dens, src, tgt, ids), s[14:18])
        firsts.append([pltpu.make_async_copy(a, v, s[13].at[i]) for i, (a, v) in enumerate(moves)])
    for i in range(4):
        for first in firsts:
            first[i].start()

    barrier = pltpu.get_barrier_semaphore()
    for step in range(1, nd):
        pl.semaphore_signal(barrier, inc=1, device_id=(b, lax.rem(d + step, nd)), device_id_type=MESH)

    @pl.when(b > 0)
    def _():
        pl.semaphore_signal(barrier, inc=1, device_id=(b - 1, d), device_id_type=MESH)

    @pl.when(b < nb - 1)
    def _():
        pl.semaphore_signal(barrier, inc=1, device_id=(b + 1, d), device_id_type=MESH)

    tables = []
    for lv, (_, oper, *_), s in zip(levels, data, sets):
        tables.append(operator_copies(lv, oper, s[8], s[11]))
        for load in tables[-1]:
            load.start()

    for lv, (_, _, bal, *_), s, first in zip(levels, data, sets, firsts):
        first[0].wait()
        sort_slots(lv, nd, s[14], bal, s[0], s[1])

    jobs = []
    for lv, s, waits in zip(levels, sets, firsts):
        src, tgt, ids = s[15:18]
        lefts, rights, counts = s[4], s[5], s[6]
        for wait in waits[1:]:
            wait.wait()
        for j in range(lv.slots):
            left, right = lefts.at[j % 2], rights.at[j % 2]
            jobs.append(
                (
                    functools.partial(hot_pieces, lv, b, j, src, tgt, ids, left, right),
                    functools.partial(count_pieces, lv, j, left, right, counts),
                )
            )
    for act in jobs[0][0]():
        act()

    sides = (b > 0).astype(jnp.int32) + (b < nb - 1).astype(jnp.int32)
    pl.semaphore_wait(barrier, nd - 1 + sides)
    swaps, halos = [], []
    for lv, s in zip(levels, sets):
        swaps.append(exchange(lv, nd, b, d, s[1], s[2], s[9], s[10]))
        for swap in swaps[-1]:
            swap.start()
    for lv, s in zip(levels, sets):
        halos.append(halo_copies(lv, nd, nb, b, d, s[2], s[19]))
        send, ext, table = s[1], s[2], s[8]
        ext[lv.halo + d] = send[d]
        blank = jnp.zeros(ext.shape[1:], BF16)

        @pl.when(b == 0)
        def _():
            for i in range(lv.halo):
                ext[i] = blank

        @pl.when(b == nb - 1)
        def _():
            for i in range(lv.halo):
                ext[lv.halo + nd + i] = blank

        hole = jnp.zeros((lv.wide - lv.channel, lv.wide), BF16)
        for parity in range(2):
            for k in range(lv.ops // 2):
                table[parity, k * lv.wide + lv.channel : (k + 1) * lv.wide, :] = hole

    def hand_halos(level):
        for swap in swaps[level]:
            swap.wait_recv()
        for sends, _, copy in halos[level]:
            pl.when(sends)(copy.start)

    after = {fine_slots - 1: 0, fine_slots + coarse_slots // 2 - 1: 1}
    for i, (_, count) in enumerate(jobs):
        interleave(jobs[i + 1][0]() if i + 1 < len(jobs) else [], count())
        if i in after:
            hand_halos(after[i])

    results = []
    for lv, (*_, out), s, halo, loads in zip(levels, data, sets, halos, tables):
        for _, receives, copy in halo:
            pl.when(receives)(copy.wait_recv)
        for load in loads:
            load.wait()
        gather_rows(lv, s[2], s[3], s[7])
        expand(lv, s[6], s[7], s[12])
        apply_operators(lv, s[12], s[8], s[18])
        results.append(pltpu.make_async_copy(s[18], out, s[13].at[4]))
        results[-1].start()

    for swap, halo in zip(swaps, halos):
        for copy in swap:
            copy.wait_send()
        for sends, _, copy in halo:
            pl.when(sends)(copy.wait_send)
    for result in results:
        result.wait()


def hand_on(one, two, out1, out2):
    out1[...] = one[...]
    out2[...] = two[...]


def scratch_of(lv, nd):
    flat = BF16 if lv.rows % 16 == 0 else F32
    width = lv.slots * lv.channel
    return [
        pltpu.VMEM((lv.wedges, lv.rows, lv.channel), BF16),
        pltpu.VMEM((nd, lv.rows, width), BF16),
        pltpu.VMEM((lv.chunks, lv.rows, width), BF16),
        pltpu.VMEM((lv.span, width), flat),
        pltpu.VMEM((2, lv.left, lv.pairs), HOT),
        pltpu.VMEM((2, lv.right, lv.pairs), HOT),
        pltpu.VMEM((lv.slots, 2, lv.left, lv.right), BF16),
        pltpu.VMEM((lv.slots, 2 if lv.rest else 1, lv.depth, lv.wide), BF16),
        pltpu.VMEM((2, lv.ops // 2 * lv.wide, lv.wide), BF16),
        pltpu.SemaphoreType.DMA((nd,)),
        pltpu.SemaphoreType.DMA((nd,)),
        pltpu.SemaphoreType.DMA((lv.ops,)),
        pltpu.VMEM((2, lv.slots, 2 * lv.targets, lv.ops // 2 * lv.wide), BF16),
        pltpu.SemaphoreType.DMA((5,)),
        pltpu.VMEM((lv.rows, lv.wedges * lv.channel), BF16),
        pltpu.VMEM((lv.slots, lv.pairs), jnp.int32),
        pltpu.VMEM((lv.slots, lv.pairs), jnp.int32),
        pltpu.VMEM((lv.slots, lv.pairs), jnp.int32),
        pltpu.VMEM((lv.targets, width), BF16),
        pltpu.SemaphoreType.DMA((4,)),
    ]


def per_device(nd, nb, *args):
    fine = Level(args[0], args[2], args[6], nd)
    coarse = Level(args[1], args[3], args[9], nd)
    levels = (fine, coarse)
    smem = pl.BlockSpec(memory_space=pltpu.SMEM)
    away = pl.BlockSpec(memory_space=pl.ANY)
    shapes = tuple(
        jax.ShapeDtypeStruct((lv.targets, lv.slots * lv.channel), BF16) for lv in levels
    )
    found = pl.pallas_call(
        functools.partial(kernel, levels, nd, nb),
        out_shape=shapes,
        in_specs=[away] * 4 + [smem] * 2 + [away] * 6,
        out_specs=(away, away),
        scratch_shapes=scratch_of(fine, nd) + scratch_of(coarse, nd),
        compiler_params=pltpu.CompilerParams(
            collective_id=0, has_side_effects=True, vmem_limit_bytes=56 * 1024 * 1024
        ),
        name="translate",
    )(*args)
    return pl.pallas_call(
        hand_on,
        out_shape=shapes,
        compiler_params=pltpu.CompilerParams(vmem_limit_bytes=60 * 1024 * 1024),
        name="hand_on",
    )(*found)


def solution(mesh):
    boxes, dirs = P(("box", "dir"), None), P("dir", "box")
    return jax.shard_map(
        functools.partial(per_device, mesh.shape["dir"], mesh.shape["box"]),
        mesh=mesh,
        in_specs=(boxes, boxes, P(), P(), P(), P()) + (dirs,) * 6,
        out_specs=(P("box", "dir"), P("box", "dir")),
        check_vma=False,
    )
```

```python
import functools

import jax
import jax.numpy as jnp
from jax import lax
from jax.experimental import pallas as pl
from jax.experimental.pallas import tpu as pltpu
from jax.sharding import PartitionSpec as P

RIM = 32
LANES = 128
BF16 = jnp.bfloat16
F32 = jnp.float32
HOT = jnp.float8_e4m3fn
MESH = pl.DeviceIdType.MESH


class Level:
    def __init__(self, density, operators, sources, nd):
        self.rows, width = density.shape
        self.channel = operators.shape[0]
        self.ops = operators.shape[1] // self.channel
        self.wedges = width // self.channel
        self.slots = self.wedges // nd
        self.targets = self.rows * nd
        self.halo = RIM // self.rows
        self.chunks = nd + 2 * self.halo
        self.span = self.targets + 2 * RIM
        self.pairs = sources.shape[1]
        self.full = self.span // LANES * LANES
        self.rest = self.span - self.full
        self.lo = 4 if self.rest else 2
        self.hi = self.ops // self.lo
        self.left = self.hi * self.targets
        self.right = self.lo * self.span
        self.depth = self.full + 2 * self.rest
        self.wide = -(-self.channel // LANES) * LANES


def one_hot_pieces(out, key, count):
    row = lax.broadcasted_iota(jnp.int32, (LANES, LANES), 0).astype(F32).astype(BF16)
    row = jnp.concatenate([row] * (key.shape[1] // LANES), axis=1)
    block = lax.shift_right_logical(key, LANES.bit_length() - 1).astype(F32).astype(BF16)
    within = jnp.bitwise_and(key, LANES - 1).astype(F32).astype(BF16)

    def piece(k):
        near = jnp.where(block == jnp.asarray(k, BF16), within, -jnp.ones((), BF16))
        hot = jnp.where(near == row, jnp.ones((), BF16), jnp.zeros((), BF16))
        out[k * LANES : (k + 1) * LANES, :] = hot.astype(out.dtype)

    return [functools.partial(piece, k) for k in range(count // LANES)]


def sort_slots(lv, nd, density, balance, split, send):
    for w in range(lv.wedges):
        split[w] = density[:, w * lv.channel : (w + 1) * lv.channel]
    for d in range(nd):
        parts = [split[balance[d * lv.slots + k]] for k in range(lv.slots)]
        send[d] = jnp.concatenate(parts, axis=1)


def direct_copies(lv, nd, nb, b, d, send, ext, sems):
    send_sem, recv_sem = sems

    def copy(to_box, to_dir, chunk, sem):
        return pltpu.make_async_remote_copy(
            src_ref=send.at[to_dir],
            dst_ref=ext.at[chunk],
            send_sem=send_sem.at[sem],
            recv_sem=recv_sem.at[chunk],
            device_id=(to_box, to_dir),
            device_id_type=MESH,
        )

    sends, receives = [], []
    for step in range(nd):
        to = lax.rem(d + step, nd)
        up = jnp.logical_and(d >= nd - lv.halo, b < nb - 1)
        down = jnp.logical_and(d < lv.halo, b > 0)
        if step:
            sends.append((None, functools.partial(copy, b, to, lv.halo + d, step)))
        sends.append((up, functools.partial(copy, b + 1, to, d - (nd - lv.halo), nd + step)))
        sends.append((down, functools.partial(copy, b - 1, to, lv.halo + nd + d, 2 * nd + step)))
    for step in range(1, nd):
        chunk = lv.halo + lax.rem(d + step, nd)
        receives.append((None, functools.partial(copy, b, d, chunk, 0)))
    for i in range(lv.halo):
        receives.append((b > 0, functools.partial(copy, b, d, i, 0)))
        receives.append((b < nb - 1, functools.partial(copy, b, d, lv.halo + nd + i, 0)))
    return sends, receives


def under(condition, act):
    if condition is None:
        act()
    else:
        pl.when(condition)(act)


def exchange(lv, nd, b, d, send, ext, send_sem, recv_sem):
    result = []
    for step in range(1, nd):
        to = lax.rem(d + step, nd)
        result.append(
            pltpu.make_async_remote_copy(
                src_ref=send.at[to],
                dst_ref=ext.at[lv.halo + d],
                send_sem=send_sem.at[step],
                recv_sem=recv_sem.at[nd - step],
                device_id=(b, to),
                device_id_type=MESH,
            )
        )
    return result


def halo_copies(lv, nd, nb, b, d, ext, sem):
    up = pltpu.make_async_remote_copy(
        src_ref=ext.at[pl.ds(nd, lv.halo)],
        dst_ref=ext.at[pl.ds(0, lv.halo)],
        send_sem=sem.at[0],
        recv_sem=sem.at[1],
        device_id=(b + 1, d),
        device_id_type=MESH,
    )
    down = pltpu.make_async_remote_copy(
        src_ref=ext.at[pl.ds(lv.halo, lv.halo)],
        dst_ref=ext.at[pl.ds(lv.halo + nd, lv.halo)],
        send_sem=sem.at[2],
        recv_sem=sem.at[3],
        device_id=(b - 1, d),
        device_id_type=MESH,
    )
    return [(b < nb - 1, b > 0, up), (b > 0, b < nb - 1, down)]


def hot_pieces(lv, b, j, sources, targets, op_ids, left, right):
    at = slice(j, j + 1)
    op = op_ids[at, :]
    high = lax.shift_right_logical(op, lv.lo.bit_length() - 1)
    low = jnp.bitwise_and(op, lv.lo - 1)
    source = sources[at, :] - (b * lv.targets - RIM)
    target = targets[at, :] - b * lv.targets
    key = low * lv.full + source
    if lv.rest:
        tail = lv.lo * lv.full + low * lv.rest + (source - lv.full)
        key = jnp.where(source < lv.full, key, tail)
    return one_hot_pieces(left, high * lv.targets + target, lv.left) + one_hot_pieces(
        right, key, lv.right
    )


def count_pieces(lv, j, left, right, counts):
    def piece(columns):
        found = lax.dot_general(
            left[...], right[columns, :], (((1,), (1,)), ((), ())), preferred_element_type=F32
        )
        main = found.astype(BF16)
        counts[j, 0, :, columns] = main
        counts[j, 1, :, columns] = (found - main.astype(F32)).astype(BF16)

    step = 2 * LANES
    return [functools.partial(piece, slice(c, c + step)) for c in range(0, lv.right, step)]


def interleave(first, second):
    done = 0
    for i, act in enumerate(second):
        until = (i + 1) * len(first) // len(second)
        for other in first[done:until]:
            other()
        done = until
        act()
    for other in first[done:]:
        other()


def gather_rows(lv, ext, flat, weights):
    for q in range(lv.chunks):
        flat[q * lv.rows : (q + 1) * lv.rows, :] = ext[q].astype(flat.dtype)
    for j in range(lv.slots):
        mine = flat[:, j * lv.channel : (j + 1) * lv.channel].astype(BF16)
        pad = jnp.zeros((lv.span, lv.wide - lv.channel), BF16)
        mine = jnp.concatenate([mine, pad], axis=1)
        if lv.rest:
            none = jnp.zeros((lv.rest, lv.wide), BF16)
            weights[j, 0] = jnp.concatenate([mine, none], axis=0)
            weights[j, 1] = jnp.concatenate([mine[: lv.full], none, mine[lv.full :]], axis=0)
        else:
            weights[j, 0] = mine


def expand(lv, counts, weights, grown):
    def body(j):
        for low in range(lv.lo):
            picked = []
            for term in range(2):
                for k in range(lv.full // LANES):
                    first = low * lv.full + k * LANES
                    picked.append(counts[j, term, :, first : first + LANES])
                if lv.rest:
                    first = lv.lo * lv.full + (low // 2) * LANES
                    picked.append(counts[j, term, :, first : first + LANES])
            weight = weights[j, low % 2 if lv.rest else 0]
            total = jnp.dot(
                jnp.concatenate(picked, axis=1),
                jnp.concatenate([weight, weight], axis=0),
                preferred_element_type=F32,
            )
            main = total.astype(BF16)
            rest = (total - main.astype(F32)).astype(BF16)
            for high in range(lv.hi):
                op = high * lv.lo + low
                column = op // 2 * lv.wide
                rows = slice(high * lv.targets, (high + 1) * lv.targets)
                grown[op % 2, j, : lv.targets, column : column + lv.wide] = main[rows]
                grown[op % 2, j, lv.targets :, column : column + lv.wide] = rest[rows]

    for j in range(lv.slots):
        body(j)


def apply_operators(lv, grown, table, out):
    height = lv.slots * 2 * lv.targets
    total = []
    for parity in range(2):
        total.append(
            jnp.dot(
                grown[parity].reshape(height, grown.shape[-1]),
                table[parity],
                preferred_element_type=F32,
            )
        )
    shift = lv.wide - lv.channel
    both = total[0][:, : lv.channel] + total[1][:, shift:]
    parts = []
    for j in range(lv.slots):
        first = j * 2 * lv.targets
        part = both[first : first + lv.targets] + both[first + lv.targets : first + 2 * lv.targets]
        parts.append(part.astype(BF16))
    out[...] = jnp.concatenate(parts, axis=1)


def operator_copies(lv, operators, table, sem):
    shift = lv.wide - lv.channel
    result = []
    for op in range(lv.ops):
        first = op * lv.channel - (op % 2) * shift
        result.append(
            pltpu.make_async_copy(
                operators.at[:, pl.ds(first, lv.wide)],
                table.at[op % 2, pl.ds(op // 2 * lv.wide, lv.channel), :],
                sem.at[op],
            )
        )
    return result


def kernel(levels, nd, nb, *refs):
    (dens1, dens2, oper1, oper2, bal1, bal2, src1, tgt1, ids1, src2, tgt2, ids2, out1, out2) = refs[:14]
    scratch = refs[14:]
    per = len(scratch) // 2
    sets = (scratch[:per], scratch[per:])
    data = (
        (dens1, oper1, bal1, src1, tgt1, ids1, out1),
        (dens2, oper2, bal2, src2, tgt2, ids2, out2),
    )
    fine_slots = levels[0].slots
    b, d = lax.axis_index("box"), lax.axis_index("dir")

    firsts = []
    for (dens, _, _, src, tgt, ids, _), s in zip(data, sets):
        moves = zip((dens, src, tgt, ids), s[14:18])
        firsts.append([pltpu.make_async_copy(a, v, s[13].at[i]) for i, (a, v) in enumerate(moves)])
    for i in range(4):
        for first in firsts:
            first[i].start()

    barrier = pltpu.get_barrier_semaphore()
    for step in range(1, nd):
        pl.semaphore_signal(barrier, inc=1, device_id=(b, lax.rem(d + step, nd)), device_id_type=MESH)

    @pl.when(b > 0)
    def _():
        for to in range(nd):
            pl.semaphore_signal(barrier, inc=1, device_id=(b - 1, to), device_id_type=MESH)

    @pl.when(b < nb - 1)
    def _():
        for to in range(nd):
            pl.semaphore_signal(barrier, inc=1, device_id=(b + 1, to), device_id_type=MESH)

    tables = []
    for lv, (_, oper, *_), s in zip(levels, data, sets):
        tables.append(operator_copies(lv, oper, s[8], s[11]))
        for load in tables[-1]:
            load.start()

    for lv, (_, _, bal, *_), s, first in zip(levels, data, sets, firsts):
        first[0].wait()
        sort_slots(lv, nd, s[14], bal, s[0], s[1])

    sides = 1 + (b > 0).astype(jnp.int32) + (b < nb - 1).astype(jnp.int32)
    pl.semaphore_wait(barrier, sides * nd - 1)
    fine, coarse = levels
    s = sets[0]
    sends, receives = direct_copies(fine, nd, nb, b, d, s[1], s[2], (s[9], s[10]))
    for condition, make in sends:
        under(condition, lambda make=make: make().start())
    s = sets[1]
    swaps = exchange(coarse, nd, b, d, s[1], s[2], s[9], s[10])
    for swap in swaps:
        swap.start()
    halos = halo_copies(coarse, nd, nb, b, d, s[2], s[19])
    for lv, s in zip(levels, sets):
        send, ext, table = s[1], s[2], s[8]
        ext[lv.halo + d] = send[d]
        blank = jnp.zeros(ext.shape[1:], BF16)

        @pl.when(b == 0)
        def _():
            for i in range(lv.halo):
                ext[i] = blank

        @pl.when(b == nb - 1)
        def _():
            for i in range(lv.halo):
                ext[lv.halo + nd + i] = blank

        hole = jnp.zeros((lv.wide - lv.channel, lv.wide), BF16)
        for parity in range(2):
            for k in range(lv.ops // 2):
                table[parity, k * lv.wide + lv.channel : (k + 1) * lv.wide, :] = hole

    jobs = []
    for lv, s, waits in zip(levels, sets, firsts):
        src, tgt, ids = s[15:18]
        lefts, rights, counts = s[4], s[5], s[6]
        for wait in waits[1:]:
            wait.wait()
        for j in range(lv.slots):
            left, right = lefts.at[j % 2], rights.at[j % 2]
            jobs.append(
                (
                    functools.partial(hot_pieces, lv, b, j, src, tgt, ids, left, right),
                    functools.partial(count_pieces, lv, j, left, right, counts),
                )
            )
    for act in jobs[0][0]():
        act()

    def hand_halos():
        for swap in swaps:
            swap.wait_recv()
        for gives, _, copy in halos:
            pl.when(gives)(copy.start)

    def wait_fine():
        for condition, make in receives:
            under(condition, lambda make=make: make().wait_recv())

    def wait_coarse():
        for _, takes, copy in halos:
            pl.when(takes)(copy.wait_recv)

    for i, (_, count) in enumerate(jobs):
        interleave(jobs[i + 1][0]() if i + 1 < len(jobs) else [], count())
        if i == fine_slots:
            hand_halos()

    results = []
    for lv, (*_, out), s, loads, arrive in zip(
        levels, data, sets, tables, (wait_fine, wait_coarse)
    ):
        arrive()
        for load in loads:
            load.wait()
        gather_rows(lv, s[2], s[3], s[7])
        expand(lv, s[6], s[7], s[12])
        apply_operators(lv, s[12], s[8], s[18])
        results.append(pltpu.make_async_copy(s[18], out, s[13].at[4]))
        results[-1].start()

    for condition, make in sends:
        under(condition, lambda make=make: make().wait_send())
    for swap in swaps:
        swap.wait_send()
    for gives, _, copy in halos:
        pl.when(gives)(copy.wait_send)
    for result in results:
        result.wait()


def hand_on(one, two, out1, out2):
    out1[...] = one[...]
    out2[...] = two[...]


def scratch_of(lv, nd):
    flat = BF16 if lv.rows % 16 == 0 else F32
    width = lv.slots * lv.channel
    return [
        pltpu.VMEM((lv.wedges, lv.rows, lv.channel), BF16),
        pltpu.VMEM((nd, lv.rows, width), BF16),
        pltpu.VMEM((lv.chunks, lv.rows, width), BF16),
        pltpu.VMEM((lv.span, width), flat),
        pltpu.VMEM((2, lv.left, lv.pairs), HOT),
        pltpu.VMEM((2, lv.right, lv.pairs), HOT),
        pltpu.VMEM((lv.slots, 2, lv.left, lv.right), BF16),
        pltpu.VMEM((lv.slots, 2 if lv.rest else 1, lv.depth, lv.wide), BF16),
        pltpu.VMEM((2, lv.ops // 2 * lv.wide, lv.wide), BF16),
        pltpu.SemaphoreType.DMA((3 * nd,)),
        pltpu.SemaphoreType.DMA((lv.chunks,)),
        pltpu.SemaphoreType.DMA((lv.ops,)),
        pltpu.VMEM((2, lv.slots, 2 * lv.targets, lv.ops // 2 * lv.wide), BF16),
        pltpu.SemaphoreType.DMA((5,)),
        pltpu.VMEM((lv.rows, lv.wedges * lv.channel), BF16),
        pltpu.VMEM((lv.slots, lv.pairs), jnp.int32),
        pltpu.VMEM((lv.slots, lv.pairs), jnp.int32),
        pltpu.VMEM((lv.slots, lv.pairs), jnp.int32),
        pltpu.VMEM((lv.targets, width), BF16),
        pltpu.SemaphoreType.DMA((4,)),
    ]


def per_device(nd, nb, *args):
    fine = Level(args[0], args[2], args[6], nd)
    coarse = Level(args[1], args[3], args[9], nd)
    levels = (fine, coarse)
    smem = pl.BlockSpec(memory_space=pltpu.SMEM)
    away = pl.BlockSpec(memory_space=pl.ANY)
    shapes = tuple(
        jax.ShapeDtypeStruct((lv.targets, lv.slots * lv.channel), BF16) for lv in levels
    )
    found = pl.pallas_call(
        functools.partial(kernel, levels, nd, nb),
        out_shape=shapes,
        in_specs=[away] * 4 + [smem] * 2 + [away] * 6,
        out_specs=(away, away),
        scratch_shapes=scratch_of(fine, nd) + scratch_of(coarse, nd),
        compiler_params=pltpu.CompilerParams(
            collective_id=0, has_side_effects=True, vmem_limit_bytes=56 * 1024 * 1024
        ),
        name="translate",
    )(*args)
    return pl.pallas_call(
        hand_on,
        out_shape=shapes,
        compiler_params=pltpu.CompilerParams(vmem_limit_bytes=60 * 1024 * 1024),
        name="hand_on",
    )(*found)


def solution(mesh):
    boxes, dirs = P(("box", "dir"), None), P("dir", "box")
    return jax.shard_map(
        functools.partial(per_device, mesh.shape["dir"], mesh.shape["box"]),
        mesh=mesh,
        in_specs=(boxes, boxes, P(), P(), P(), P()) + (dirs,) * 6,
        out_specs=(P("box", "dir"), P("box", "dir")),
        check_vma=False,
    )
```

```python
import functools

import jax
import jax.numpy as jnp
from jax import lax
from jax.experimental import pallas as pl
from jax.experimental.pallas import tpu as pltpu
from jax.sharding import PartitionSpec as P

RIM = 32
LANES = 128
BF16 = jnp.bfloat16
F32 = jnp.float32
HOT = jnp.float8_e4m3fn
MESH = pl.DeviceIdType.MESH


class Level:
    def __init__(self, density, operators, sources, nd):
        self.rows, width = density.shape
        self.channel = operators.shape[0]
        self.ops = operators.shape[1] // self.channel
        self.wedges = width // self.channel
        self.slots = self.wedges // nd
        self.targets = self.rows * nd
        self.halo = RIM // self.rows
        self.chunks = nd + 2 * self.halo
        self.span = self.targets + 2 * RIM
        self.pairs = sources.shape[1]
        self.full = self.span // LANES * LANES
        self.rest = self.span - self.full
        self.lo = 4 if self.rest else 2
        self.hi = self.ops // self.lo
        self.left = self.hi * self.targets
        self.right = self.lo * self.span
        self.depth = self.full + 2 * self.rest
        self.wide = -(-self.channel // LANES) * LANES


def one_hot_pieces(out, key, count):
    row = lax.broadcasted_iota(jnp.int32, (LANES, LANES), 0).astype(F32).astype(BF16)
    row = jnp.concatenate([row] * (key.shape[1] // LANES), axis=1)
    block = lax.shift_right_logical(key, LANES.bit_length() - 1).astype(F32).astype(BF16)
    within = jnp.bitwise_and(key, LANES - 1).astype(F32).astype(BF16)

    def piece(k):
        near = jnp.where(block == jnp.asarray(k, BF16), within, -jnp.ones((), BF16))
        hot = jnp.where(near == row, jnp.ones((), BF16), jnp.zeros((), BF16))
        out[k * LANES : (k + 1) * LANES, :] = hot.astype(out.dtype)

    return [functools.partial(piece, k) for k in range(count // LANES)]


def sort_slots(lv, nd, density, balance, split, send):
    for w in range(lv.wedges):
        split[w] = density[:, w * lv.channel : (w + 1) * lv.channel]
    for d in range(nd):
        parts = [split[balance[d * lv.slots + k]] for k in range(lv.slots)]
        send[d] = jnp.concatenate(parts, axis=1)


def copies(lv, nd, nb, b, d, send, ext, sems):
    send_sem, recv_sem = sems

    def copy(to_box, to_dir, chunk, sem):
        return pltpu.make_async_remote_copy(
            src_ref=send.at[to_dir],
            dst_ref=ext.at[chunk],
            send_sem=send_sem.at[sem],
            recv_sem=recv_sem.at[chunk],
            device_id=(to_box, to_dir),
            device_id_type=MESH,
        )

    sends, receives = [], []
    for step in range(nd):
        to = lax.rem(d + step, nd)
        up = jnp.logical_and(d >= nd - lv.halo, b < nb - 1)
        down = jnp.logical_and(d < lv.halo, b > 0)
        if step:
            sends.append((None, functools.partial(copy, b, to, lv.halo + d, step)))
        sends.append((up, functools.partial(copy, b + 1, to, d - (nd - lv.halo), nd + step)))
        sends.append((down, functools.partial(copy, b - 1, to, lv.halo + nd + d, 2 * nd + step)))
    for step in range(1, nd):
        chunk = lv.halo + lax.rem(d + step, nd)
        receives.append((None, functools.partial(copy, b, d, chunk, 0)))
    for i in range(lv.halo):
        receives.append((b > 0, functools.partial(copy, b, d, i, 0)))
        receives.append((b < nb - 1, functools.partial(copy, b, d, lv.halo + nd + i, 0)))
    return sends, receives


def under(condition, act):
    if condition is None:
        act()
    else:
        pl.when(condition)(act)


def hot_pieces(lv, b, j, sources, targets, op_ids, left, right):
    at = slice(j, j + 1)
    op = op_ids[at, :]
    high = lax.shift_right_logical(op, lv.lo.bit_length() - 1)
    low = jnp.bitwise_and(op, lv.lo - 1)
    source = sources[at, :] - (b * lv.targets - RIM)
    target = targets[at, :] - b * lv.targets
    key = low * lv.full + source
    if lv.rest:
        tail = lv.lo * lv.full + low * lv.rest + (source - lv.full)
        key = jnp.where(source < lv.full, key, tail)
    return one_hot_pieces(left, high * lv.targets + target, lv.left) + one_hot_pieces(
        right, key, lv.right
    )


def count_pieces(lv, j, left, right, counts):
    def piece(columns):
        found = lax.dot_general(
            left[...], right[columns, :], (((1,), (1,)), ((), ())), preferred_element_type=F32
        )
        main = found.astype(BF16)
        counts[j, 0, :, columns] = main
        counts[j, 1, :, columns] = (found - main.astype(F32)).astype(BF16)

    step = 2 * LANES
    return [functools.partial(piece, slice(c, c + step)) for c in range(0, lv.right, step)]


def interleave(first, second):
    done = 0
    for i, act in enumerate(second):
        until = (i + 1) * len(first) // len(second)
        for other in first[done:until]:
            other()
        done = until
        act()
    for other in first[done:]:
        other()


def gather_rows(lv, ext, flat, weights):
    for q in range(lv.chunks):
        flat[q * lv.rows : (q + 1) * lv.rows, :] = ext[q].astype(flat.dtype)
    for j in range(lv.slots):
        mine = flat[:, j * lv.channel : (j + 1) * lv.channel].astype(BF16)
        pad = jnp.zeros((lv.span, lv.wide - lv.channel), BF16)
        mine = jnp.concatenate([mine, pad], axis=1)
        if lv.rest:
            none = jnp.zeros((lv.rest, lv.wide), BF16)
            weights[j, 0] = jnp.concatenate([mine, none], axis=0)
            weights[j, 1] = jnp.concatenate([mine[: lv.full], none, mine[lv.full :]], axis=0)
        else:
            weights[j, 0] = mine


def expand(lv, counts, weights, grown):
    def body(j):
        for low in range(lv.lo):
            picked = []
            for term in range(2):
                for k in range(lv.full // LANES):
                    first = low * lv.full + k * LANES
                    picked.append(counts[j, term, :, first : first + LANES])
                if lv.rest:
                    first = lv.lo * lv.full + (low // 2) * LANES
                    picked.append(counts[j, term, :, first : first + LANES])
            weight = weights[j, low % 2 if lv.rest else 0]
            total = jnp.dot(
                jnp.concatenate(picked, axis=1),
                jnp.concatenate([weight, weight], axis=0),
                preferred_element_type=F32,
            )
            main = total.astype(BF16)
            rest = (total - main.astype(F32)).astype(BF16)
            for high in range(lv.hi):
                op = high * lv.lo + low
                column = op // 2 * lv.wide
                rows = slice(high * lv.targets, (high + 1) * lv.targets)
                grown[op % 2, j, : lv.targets, column : column + lv.wide] = main[rows]
                grown[op % 2, j, lv.targets :, column : column + lv.wide] = rest[rows]

    for j in range(lv.slots):
        body(j)


def apply_operators(lv, grown, table, out):
    height = lv.slots * 2 * lv.targets
    total = []
    for parity in range(2):
        total.append(
            jnp.dot(
                grown[parity].reshape(height, grown.shape[-1]),
                table[parity],
                preferred_element_type=F32,
            )
        )
    shift = lv.wide - lv.channel
    both = total[0][:, : lv.channel] + total[1][:, shift:]
    parts = []
    for j in range(lv.slots):
        first = j * 2 * lv.targets
        part = both[first : first + lv.targets] + both[first + lv.targets : first + 2 * lv.targets]
        parts.append(part.astype(BF16))
    out[...] = jnp.concatenate(parts, axis=1)


def operator_copies(lv, operators, table, sem):
    shift = lv.wide - lv.channel
    result = []
    for op in range(lv.ops):
        first = op * lv.channel - (op % 2) * shift
        result.append(
            pltpu.make_async_copy(
                operators.at[:, pl.ds(first, lv.wide)],
                table.at[op % 2, pl.ds(op // 2 * lv.wide, lv.channel), :],
                sem.at[op],
            )
        )
    return result


def kernel(levels, nd, nb, *refs):
    (dens1, dens2, oper1, oper2, bal1, bal2, src1, tgt1, ids1, src2, tgt2, ids2, out1, out2) = refs[:14]
    scratch = refs[14:]
    per = len(scratch) // 2
    sets = (scratch[:per], scratch[per:])
    data = (
        (dens1, oper1, bal1, src1, tgt1, ids1, out1),
        (dens2, oper2, bal2, src2, tgt2, ids2, out2),
    )
    b, d = lax.axis_index("box"), lax.axis_index("dir")

    firsts = []
    for (dens, _, _, src, tgt, ids, _), s in zip(data, sets):
        moves = zip((dens, src, tgt, ids), s[14:18])
        firsts.append([pltpu.make_async_copy(a, v, s[13].at[i]) for i, (a, v) in enumerate(moves)])
    for i in range(4):
        for first in firsts:
            first[i].start()

    barrier = pltpu.get_barrier_semaphore()
    for step in range(1, nd):
        pl.semaphore_signal(barrier, inc=1, device_id=(b, lax.rem(d + step, nd)), device_id_type=MESH)

    @pl.when(b > 0)
    def _():
        for to in range(nd):
            pl.semaphore_signal(barrier, inc=1, device_id=(b - 1, to), device_id_type=MESH)

    @pl.when(b < nb - 1)
    def _():
        for to in range(nd):
            pl.semaphore_signal(barrier, inc=1, device_id=(b + 1, to), device_id_type=MESH)

    for lv, s in zip(levels, sets):
        ext, table = s[2], s[8]
        blank = jnp.zeros(ext.shape[1:], BF16)

        @pl.when(b == 0)
        def _():
            for i in range(lv.halo):
                ext[i] = blank

        @pl.when(b == nb - 1)
        def _():
            for i in range(lv.halo):
                ext[lv.halo + nd + i] = blank

        hole = jnp.zeros((lv.wide - lv.channel, lv.wide), BF16)
        for parity in range(2):
            for k in range(lv.ops // 2):
                table[parity, k * lv.wide + lv.channel : (k + 1) * lv.wide, :] = hole

    plans = []
    for at, (lv, (_, _, bal, *_), s, first) in enumerate(zip(levels, data, sets, firsts)):
        first[0].wait()
        sort_slots(lv, nd, s[14], bal, s[0], s[1])
        if at == 0:
            sides = 1 + (b > 0).astype(jnp.int32) + (b < nb - 1).astype(jnp.int32)
            pl.semaphore_wait(barrier, sides * nd - 1)
        send, ext = s[1], s[2]
        sends, receives = copies(lv, nd, nb, b, d, send, ext, (s[9], s[10]))
        plans.append((sends, receives))
        for condition, make in sends:
            under(condition, lambda make=make: make().start())
    tables = []
    for lv, (_, oper, *_), s in zip(levels, data, sets):
        tables.append(operator_copies(lv, oper, s[8], s[11]))
    for load in tables[0]:
        load.start()

    jobs = []
    for lv, s, waits in zip(levels, sets, firsts):
        src, tgt, ids = s[15:18]
        send, ext, lefts, rights, counts = s[1], s[2], s[4], s[5], s[6]
        for wait in waits[1:]:
            wait.wait()
        ext[lv.halo + d] = send[d]
        for j in range(lv.slots):
            left, right = lefts.at[j % 2], rights.at[j % 2]
            jobs.append(
                (
                    functools.partial(hot_pieces, lv, b, j, src, tgt, ids, left, right),
                    functools.partial(count_pieces, lv, j, left, right, counts),
                )
            )

    for act in jobs[0][0]():
        act()
    for i, (_, count) in enumerate(jobs):
        interleave(jobs[i + 1][0]() if i + 1 < len(jobs) else [], count())
        if i == 0:
            for load in tables[1]:
                load.start()

    results = []
    for lv, (*_, out), s, (_, receives), loads in zip(levels, data, sets, plans, tables):
        for condition, make in receives:
            under(condition, lambda make=make: make().wait_recv())
        for load in loads:
            load.wait()
        gather_rows(lv, s[2], s[3], s[7])
        expand(lv, s[6], s[7], s[12])
        apply_operators(lv, s[12], s[8], s[18])
        results.append(pltpu.make_async_copy(s[18], out, s[13].at[4]))
        results[-1].start()

    for sends, receives in plans:
        for condition, make in sends:
            under(condition, lambda make=make: make().wait_send())
    for result in results:
        result.wait()


def hand_on(one, two, out1, out2):
    out1[...] = one[...]
    out2[...] = two[...]


def scratch_of(lv, nd):
    flat = BF16 if lv.rows % 16 == 0 else F32
    width = lv.slots * lv.channel
    return [
        pltpu.VMEM((lv.wedges, lv.rows, lv.channel), BF16),
        pltpu.VMEM((nd, lv.rows, width), BF16),
        pltpu.VMEM((lv.chunks, lv.rows, width), BF16),
        pltpu.VMEM((lv.span, width), flat),
        pltpu.VMEM((2, lv.left, lv.pairs), HOT),
        pltpu.VMEM((2, lv.right, lv.pairs), HOT),
        pltpu.VMEM((lv.slots, 2, lv.left, lv.right), BF16),
        pltpu.VMEM((lv.slots, 2 if lv.rest else 1, lv.depth, lv.wide), BF16),
        pltpu.VMEM((2, lv.ops // 2 * lv.wide, lv.wide), BF16),
        pltpu.SemaphoreType.DMA((3 * nd,)),
        pltpu.SemaphoreType.DMA((lv.chunks,)),
        pltpu.SemaphoreType.DMA((lv.ops,)),
        pltpu.VMEM((2, lv.slots, 2 * lv.targets, lv.ops // 2 * lv.wide), BF16),
        pltpu.SemaphoreType.DMA((5,)),
        pltpu.VMEM((lv.rows, lv.wedges * lv.channel), BF16),
        pltpu.VMEM((lv.slots, lv.pairs), jnp.int32),
        pltpu.VMEM((lv.slots, lv.pairs), jnp.int32),
        pltpu.VMEM((lv.slots, lv.pairs), jnp.int32),
        pltpu.VMEM((lv.targets, width), BF16),
    ]


def per_device(nd, nb, *args):
    fine = Level(args[0], args[2], args[6], nd)
    coarse = Level(args[1], args[3], args[9], nd)
    levels = (fine, coarse)
    smem = pl.BlockSpec(memory_space=pltpu.SMEM)
    away = pl.BlockSpec(memory_space=pl.ANY)
    shapes = tuple(
        jax.ShapeDtypeStruct((lv.targets, lv.slots * lv.channel), BF16) for lv in levels
    )
    found = pl.pallas_call(
        functools.partial(kernel, levels, nd, nb),
        out_shape=shapes,
        in_specs=[away] * 4 + [smem] * 2 + [away] * 6,
        out_specs=(away, away),
        scratch_shapes=scratch_of(fine, nd) + scratch_of(coarse, nd),
        compiler_params=pltpu.CompilerParams(
            collective_id=0, has_side_effects=True, vmem_limit_bytes=56 * 1024 * 1024
        ),
        name="translate",
    )(*args)
    return pl.pallas_call(
        hand_on,
        out_shape=shapes,
        compiler_params=pltpu.CompilerParams(vmem_limit_bytes=60 * 1024 * 1024),
        name="hand_on",
    )(*found)


def solution(mesh):
    boxes, dirs = P(("box", "dir"), None), P("dir", "box")
    return jax.shard_map(
        functools.partial(per_device, mesh.shape["dir"], mesh.shape["box"]),
        mesh=mesh,
        in_specs=(boxes, boxes, P(), P(), P(), P()) + (dirs,) * 6,
        out_specs=(P("box", "dir"), P("box", "dir")),
        check_vma=False,
    )
```

```python
import functools

import jax
import jax.numpy as jnp
from jax import lax
from jax.experimental import pallas as pl
from jax.experimental.pallas import tpu as pltpu
from jax.sharding import PartitionSpec as P

RIM = 32
LANES = 128
BF16 = jnp.bfloat16
F32 = jnp.float32
HOT = jnp.float8_e4m3fn
MESH = pl.DeviceIdType.MESH


class Level:
    def __init__(self, density, operators, sources, nd):
        self.rows, width = density.shape
        self.channel = operators.shape[0]
        self.ops = operators.shape[1] // self.channel
        self.wedges = width // self.channel
        self.slots = self.wedges // nd
        self.targets = self.rows * nd
        self.halo = RIM // self.rows
        self.chunks = nd + 2 * self.halo
        self.span = self.targets + 2 * RIM
        self.pairs = sources.shape[1]
        self.full = self.span // LANES * LANES
        self.rest = self.span - self.full
        self.lo = 4 if self.rest else 2
        self.hi = self.ops // self.lo
        self.left = self.hi * self.targets
        self.right = self.lo * self.span
        self.depth = self.full + 2 * self.rest
        self.wide = -(-self.channel // LANES) * LANES


def one_hot_pieces(out, key, count):
    row = lax.broadcasted_iota(jnp.int32, (LANES, LANES), 0).astype(F32).astype(BF16)
    row = jnp.concatenate([row] * (key.shape[1] // LANES), axis=1)
    block = lax.shift_right_logical(key, LANES.bit_length() - 1).astype(F32).astype(BF16)
    within = jnp.bitwise_and(key, LANES - 1).astype(F32).astype(BF16)

    def piece(k):
        near = jnp.where(block == jnp.asarray(k, BF16), within, -jnp.ones((), BF16))
        hot = jnp.where(near == row, jnp.ones((), BF16), jnp.zeros((), BF16))
        out[k * LANES : (k + 1) * LANES, :] = hot.astype(out.dtype)

    return [functools.partial(piece, k) for k in range(count // LANES)]


def sort_slots(lv, nd, density, balance, split, send):
    for w in range(lv.wedges):
        split[w] = density[:, w * lv.channel : (w + 1) * lv.channel]
    for d in range(nd):
        parts = [split[balance[d * lv.slots + k]] for k in range(lv.slots)]
        send[d] = jnp.concatenate(parts, axis=1)


def copies(lv, nd, nb, b, d, send, ext, sems):
    send_sem, recv_sem = sems

    def copy(to_box, to_dir, chunk, sem):
        return pltpu.make_async_remote_copy(
            src_ref=send.at[to_dir],
            dst_ref=ext.at[chunk],
            send_sem=send_sem.at[sem],
            recv_sem=recv_sem.at[chunk],
            device_id=(to_box, to_dir),
            device_id_type=MESH,
        )

    sends, receives = [], []
    for step in range(nd):
        to = lax.rem(d + step, nd)
        up = jnp.logical_and(d >= nd - lv.halo, b < nb - 1)
        down = jnp.logical_and(d < lv.halo, b > 0)
        sends.append((up, functools.partial(copy, b + 1, to, d - (nd - lv.halo), nd + step)))
        sends.append((down, functools.partial(copy, b - 1, to, lv.halo + nd + d, 2 * nd + step)))
    for step in range(1, nd):
        to = lax.rem(d + step, nd)
        sends.append((None, functools.partial(copy, b, to, lv.halo + d, step)))
    for step in range(1, nd):
        chunk = lv.halo + lax.rem(d + step, nd)
        receives.append((None, functools.partial(copy, b, d, chunk, 0)))
    for i in range(lv.halo):
        receives.append((b > 0, functools.partial(copy, b, d, i, 0)))
        receives.append((b < nb - 1, functools.partial(copy, b, d, lv.halo + nd + i, 0)))
    return sends, receives


def under(condition, act):
    if condition is None:
        act()
    else:
        pl.when(condition)(act)


def hot_pieces(lv, b, j, sources, targets, op_ids, left, right):
    at = slice(j, j + 1)
    op = op_ids[at, :]
    high = lax.shift_right_logical(op, lv.lo.bit_length() - 1)
    low = jnp.bitwise_and(op, lv.lo - 1)
    source = sources[at, :] - (b * lv.targets - RIM)
    target = targets[at, :] - b * lv.targets
    key = low * lv.full + source
    if lv.rest:
        tail = lv.lo * lv.full + low * lv.rest + (source - lv.full)
        key = jnp.where(source < lv.full, key, tail)
    return one_hot_pieces(left, high * lv.targets + target, lv.left) + one_hot_pieces(
        right, key, lv.right
    )


def count_pieces(lv, j, left, right, counts):
    def piece(columns):
        found = lax.dot_general(
            left[...], right[columns, :], (((1,), (1,)), ((), ())), preferred_element_type=F32
        )
        main = found.astype(BF16)
        counts[j, 0, :, columns] = main
        counts[j, 1, :, columns] = (found - main.astype(F32)).astype(BF16)

    step = 2 * LANES
    return [functools.partial(piece, slice(c, c + step)) for c in range(0, lv.right, step)]


def interleave(first, second):
    done = 0
    for i, act in enumerate(second):
        until = (i + 1) * len(first) // len(second)
        for other in first[done:until]:
            other()
        done = until
        act()
    for other in first[done:]:
        other()


def gather_rows(lv, ext, flat, weights):
    for q in range(lv.chunks):
        flat[q * lv.rows : (q + 1) * lv.rows, :] = ext[q].astype(flat.dtype)
    for j in range(lv.slots):
        mine = flat[:, j * lv.channel : (j + 1) * lv.channel].astype(BF16)
        pad = jnp.zeros((lv.span, lv.wide - lv.channel), BF16)
        mine = jnp.concatenate([mine, pad], axis=1)
        if lv.rest:
            none = jnp.zeros((lv.rest, lv.wide), BF16)
            weights[j, 0] = jnp.concatenate([mine, none], axis=0)
            weights[j, 1] = jnp.concatenate([mine[: lv.full], none, mine[lv.full :]], axis=0)
        else:
            weights[j, 0] = mine


def expand(lv, counts, weights, grown):
    def body(j):
        for low in range(lv.lo):
            picked = []
            for term in range(2):
                for k in range(lv.full // LANES):
                    first = low * lv.full + k * LANES
                    picked.append(counts[j, term, :, first : first + LANES])
                if lv.rest:
                    first = lv.lo * lv.full + (low // 2) * LANES
                    picked.append(counts[j, term, :, first : first + LANES])
            weight = weights[j, low % 2 if lv.rest else 0]
            total = jnp.dot(
                jnp.concatenate(picked, axis=1),
                jnp.concatenate([weight, weight], axis=0),
                preferred_element_type=F32,
            )
            main = total.astype(BF16)
            rest = (total - main.astype(F32)).astype(BF16)
            for high in range(lv.hi):
                op = high * lv.lo + low
                column = op // 2 * lv.wide
                rows = slice(high * lv.targets, (high + 1) * lv.targets)
                grown[op % 2, j, : lv.targets, column : column + lv.wide] = main[rows]
                grown[op % 2, j, lv.targets :, column : column + lv.wide] = rest[rows]

    for j in range(lv.slots):
        body(j)


def apply_operators(lv, grown, table, out):
    height = lv.slots * 2 * lv.targets
    total = []
    for parity in range(2):
        total.append(
            jnp.dot(
                grown[parity].reshape(height, grown.shape[-1]),
                table[parity],
                preferred_element_type=F32,
            )
        )
    shift = lv.wide - lv.channel
    both = total[0][:, : lv.channel] + total[1][:, shift:]
    parts = []
    for j in range(lv.slots):
        first = j * 2 * lv.targets
        part = both[first : first + lv.targets] + both[first + lv.targets : first + 2 * lv.targets]
        parts.append(part.astype(BF16))
    out[...] = jnp.concatenate(parts, axis=1)


def operator_copies(lv, operators, table, sem):
    shift = lv.wide - lv.channel
    result = []
    for op in range(lv.ops):
        first = op * lv.channel - (op % 2) * shift
        result.append(
            pltpu.make_async_copy(
                operators.at[:, pl.ds(first, lv.wide)],
                table.at[op % 2, pl.ds(op // 2 * lv.wide, lv.channel), :],
                sem.at[op],
            )
        )
    return result


def kernel(levels, nd, nb, *refs):
    (dens1, dens2, oper1, oper2, bal1, bal2, src1, tgt1, ids1, src2, tgt2, ids2, out1, out2) = refs[:14]
    scratch = refs[14:]
    per = len(scratch) // 2
    sets = (scratch[:per], scratch[per:])
    data = (
        (dens1, oper1, bal1, src1, tgt1, ids1, out1),
        (dens2, oper2, bal2, src2, tgt2, ids2, out2),
    )
    b, d = lax.axis_index("box"), lax.axis_index("dir")

    firsts = []
    for (dens, _, _, src, tgt, ids, _), s in zip(data, sets):
        moves = zip((dens, src, tgt, ids), s[14:18])
        firsts.append([pltpu.make_async_copy(a, v, s[13].at[i]) for i, (a, v) in enumerate(moves)])
    for i in range(4):
        for first in firsts:
            first[i].start()

    barrier = pltpu.get_barrier_semaphore()
    for step in range(1, nd):
        pl.semaphore_signal(barrier, inc=1, device_id=(b, lax.rem(d + step, nd)), device_id_type=MESH)

    @pl.when(b > 0)
    def _():
        for to in range(nd):
            pl.semaphore_signal(barrier, inc=1, device_id=(b - 1, to), device_id_type=MESH)

    @pl.when(b < nb - 1)
    def _():
        for to in range(nd):
            pl.semaphore_signal(barrier, inc=1, device_id=(b + 1, to), device_id_type=MESH)

    for lv, s in zip(levels, sets):
        ext, table = s[2], s[8]
        blank = jnp.zeros(ext.shape[1:], BF16)

        @pl.when(b == 0)
        def _():
            for i in range(lv.halo):
                ext[i] = blank

        @pl.when(b == nb - 1)
        def _():
            for i in range(lv.halo):
                ext[lv.halo + nd + i] = blank

        hole = jnp.zeros((lv.wide - lv.channel, lv.wide), BF16)
        for parity in range(2):
            for k in range(lv.ops // 2):
                table[parity, k * lv.wide + lv.channel : (k + 1) * lv.wide, :] = hole

    plans = []
    for at, (lv, (_, _, bal, *_), s, first) in enumerate(zip(levels, data, sets, firsts)):
        first[0].wait()
        sort_slots(lv, nd, s[14], bal, s[0], s[1])
        if at == 0:
            sides = 1 + (b > 0).astype(jnp.int32) + (b < nb - 1).astype(jnp.int32)
            pl.semaphore_wait(barrier, sides * nd - 1)
        send, ext = s[1], s[2]
        sends, receives = copies(lv, nd, nb, b, d, send, ext, (s[9], s[10]))
        plans.append((sends, receives))
        for condition, make in sends:
            under(condition, lambda make=make: make().start())
    tables = []
    for lv, (_, oper, *_), s in zip(levels, data, sets):
        tables.append(operator_copies(lv, oper, s[8], s[11]))
    for load in tables[0]:
        load.start()

    jobs = []
    for lv, s, waits in zip(levels, sets, firsts):
        src, tgt, ids = s[15:18]
        send, ext, lefts, rights, counts = s[1], s[2], s[4], s[5], s[6]
        for wait in waits[1:]:
            wait.wait()
        ext[lv.halo + d] = send[d]
        for j in range(lv.slots):
            left, right = lefts.at[j % 2], rights.at[j % 2]
            jobs.append(
                (
                    functools.partial(hot_pieces, lv, b, j, src, tgt, ids, left, right),
                    functools.partial(count_pieces, lv, j, left, right, counts),
                )
            )

    for act in jobs[0][0]():
        act()
    for i, (_, count) in enumerate(jobs):
        interleave(jobs[i + 1][0]() if i + 1 < len(jobs) else [], count())
        if i == 0:
            for load in tables[1]:
                load.start()

    results = []
    for lv, (*_, out), s, (_, receives), loads in zip(levels, data, sets, plans, tables):
        for condition, make in receives:
            under(condition, lambda make=make: make().wait_recv())
        for load in loads:
            load.wait()
        gather_rows(lv, s[2], s[3], s[7])
        expand(lv, s[6], s[7], s[12])
        apply_operators(lv, s[12], s[8], s[18])
        results.append(pltpu.make_async_copy(s[18], out, s[13].at[4]))
        results[-1].start()

    for sends, receives in plans:
        for condition, make in sends:
            under(condition, lambda make=make: make().wait_send())
    for result in results:
        result.wait()


def hand_on(one, two, out1, out2):
    out1[...] = one[...]
    out2[...] = two[...]


def scratch_of(lv, nd):
    flat = BF16 if lv.rows % 16 == 0 else F32
    width = lv.slots * lv.channel
    return [
        pltpu.VMEM((lv.wedges, lv.rows, lv.channel), BF16),
        pltpu.VMEM((nd, lv.rows, width), BF16),
        pltpu.VMEM((lv.chunks, lv.rows, width), BF16),
        pltpu.VMEM((lv.span, width), flat),
        pltpu.VMEM((2, lv.left, lv.pairs), HOT),
        pltpu.VMEM((2, lv.right, lv.pairs), HOT),
        pltpu.VMEM((lv.slots, 2, lv.left, lv.right), BF16),
        pltpu.VMEM((lv.slots, 2 if lv.rest else 1, lv.depth, lv.wide), BF16),
        pltpu.VMEM((2, lv.ops // 2 * lv.wide, lv.wide), BF16),
        pltpu.SemaphoreType.DMA((3 * nd,)),
        pltpu.SemaphoreType.DMA((lv.chunks,)),
        pltpu.SemaphoreType.DMA((lv.ops,)),
        pltpu.VMEM((2, lv.slots, 2 * lv.targets, lv.ops // 2 * lv.wide), BF16),
        pltpu.SemaphoreType.DMA((5,)),
        pltpu.VMEM((lv.rows, lv.wedges * lv.channel), BF16),
        pltpu.VMEM((lv.slots, lv.pairs), jnp.int32),
        pltpu.VMEM((lv.slots, lv.pairs), jnp.int32),
        pltpu.VMEM((lv.slots, lv.pairs), jnp.int32),
        pltpu.VMEM((lv.targets, width), BF16),
    ]


def per_device(nd, nb, *args):
    fine = Level(args[0], args[2], args[6], nd)
    coarse = Level(args[1], args[3], args[9], nd)
    levels = (fine, coarse)
    smem = pl.BlockSpec(memory_space=pltpu.SMEM)
    away = pl.BlockSpec(memory_space=pl.ANY)
    shapes = tuple(
        jax.ShapeDtypeStruct((lv.targets, lv.slots * lv.channel), BF16) for lv in levels
    )
    found = pl.pallas_call(
        functools.partial(kernel, levels, nd, nb),
        out_shape=shapes,
        in_specs=[away] * 4 + [smem] * 2 + [away] * 6,
        out_specs=(away, away),
        scratch_shapes=scratch_of(fine, nd) + scratch_of(coarse, nd),
        compiler_params=pltpu.CompilerParams(
            collective_id=0, has_side_effects=True, vmem_limit_bytes=56 * 1024 * 1024
        ),
        name="translate",
    )(*args)
    return pl.pallas_call(
        hand_on,
        out_shape=shapes,
        compiler_params=pltpu.CompilerParams(vmem_limit_bytes=60 * 1024 * 1024),
        name="hand_on",
    )(*found)


def solution(mesh):
    boxes, dirs = P(("box", "dir"), None), P("dir", "box")
    return jax.shard_map(
        functools.partial(per_device, mesh.shape["dir"], mesh.shape["box"]),
        mesh=mesh,
        in_specs=(boxes, boxes, P(), P(), P(), P()) + (dirs,) * 6,
        out_specs=(P("box", "dir"), P("box", "dir")),
        check_vma=False,
    )
```
